256 devices in a mesh: dp: 32 (over x_hi, z, core), row: 2 (over x_lo), col: 4 (over y).
Axes of the slice: x: 4 (x_hi: 2, x_lo: 2; x = x_hi * 2 + x_lo), y: 4, z: 8, core: 2. Of those that a mesh axis runs over, the one named last changes fastest.
Arguments:
- out_grads: bfloat16 [40960, 4096], P('dp', 'row'), may hold values from -0.0546875 to 0.0546875
- activations: bfloat16 [40960, 4096], P('dp', 'col'), may hold values from -6 to 6
- output_factor: bfloat16 [2, 2048, 4096], P('row', 'dp'), may hold values from -1 to 4
- input_factor: bfloat16 [4096, 4096], P('col', ('dp', 'row')), may hold values from -1 to 4, as said below
Outputs:
- preconditioned: bfloat16 [4096, 4096], P('row', 'col')
The draws below stay inside these ranges and needn't reach their ends.
Inputs may be any that keep to these rules, and one draw needn't show every extreme that they name: input_factor is symmetric: entry (i, j) equals entry (j, i); and output_factor, read as a [4096, 4096] matrix (its first two dimensions joined in order), is symmetric too.
All inputs are finite; a program needn't handle non-finite values.
Results may differ from the reference program's by a relative error of at most 0.028.
Values may be sent and summed in bfloat16 or wider, within the bound.
A program may use at most 64 MiB of HBM per device.

```python
import math
import jax
import jax.numpy as jnp
from jax import lax

D_OUT = 4096
D_IN = 4096
TOK_DEV = 1280
TOKENS = 40960
N_DP = 32
N_ROW = 2


def symmetric_factor(key, order, spread, low, high):
    first, second = jax.random.split(key)
    noise = jax.random.normal(first, (order, order), jnp.float32)
    offdiag = (noise + noise.T) * (spread / math.sqrt(2.0 * order))
    diagonal = jnp.exp(jax.random.uniform(second, (order,), jnp.float32, math.log(low), math.log(high)))
    rows = lax_iota(order)
    identity = (rows[:, None] == rows[None, :]).astype(jnp.float32)
    return (offdiag + identity * diagonal[:, None]).astype(jnp.bfloat16)


def lax_iota(order):
    return jnp.arange(order, dtype=jnp.int32)


def draw_input_factor(key, part):
    key = jax.random.fold_in(key, 11)
    return symmetric_factor(key, D_IN, 0.8, 0.5, 2.0)


def draw_output_factor(key, part):
    key = jax.random.fold_in(key, 23)
    whole = symmetric_factor(key, D_OUT, 0.8, 0.5, 2.0)
    return whole.reshape(N_ROW, D_OUT // N_ROW, D_OUT)


def with_spikes(result, own_key, source, target, parts, factor):
    owner, partner = [(jnp.arange(result.shape[position]) // (result.shape[position] // parts)).reshape([-1 if axis == position else 1 for axis in range(result.ndim)]) for position in (source, target)]
    chosen = jax.random.permutation(own_key, parts)[partner]
    strong = (owner == chosen) | (owner == (partner + parts // 2) % parts)
    return jnp.where(strong, factor * result, result)


def level_of(own_key, shape, cuts, least, top_value):
    level = 1.0
    for dim, shards_of in cuts:
        draws = jax.random.uniform(jax.random.fold_in(jax.random.fold_in(own_key, 6), dim), (shards_of,), jnp.float32, least / len(cuts), top_value / len(cuts))
        level = level * jnp.repeat(jnp.exp(draws), shape[dim] // shards_of).reshape((-1,) + (1,) * (len(shape) - 1 - dim))
    return level


def normal_values(rng, extent, deviation, reach, cuts=(), kind=jnp.bfloat16):
    values = jax.random.normal(rng, extent, jnp.float32) * deviation
    if len(cuts) > 0:
        values = level_of(rng, extent, cuts, -0.22, 0.18) * values
    return jnp.clip(values, min=-reach, max=reach).astype(kind)


def heavy_noise(key, dims, deviation, reach, cuts, heavy, kind=jnp.bfloat16):
    array = deviation * jax.random.normal(key, dims, jnp.float32)
    if cuts:
        array = array * level_of(key, dims, cuts, -0.22, 0.18)
    return jnp.clip(with_spikes(array, jax.random.fold_in(key, 3), *heavy), -reach, reach).astype(kind)


def setup_inputs(seed: int = 0) -> dict:
    seeds = jax.random.split(jax.random.key(seed), 5)
    return {
        "out_grads": heavy_noise(seeds[0], (TOKENS, D_OUT), (1.0 / TOKENS ** 0.5), 0.0546875, ((0, 32), (1, 2)), (0, 1, 32, 2.75)),
        "activations": normal_values(seeds[1], (TOKENS, D_IN), 1.0, 6.0, ((0, 32), (1, 4))),
        "output_factor": draw_output_factor(jax.random.fold_in(seeds[4], 71), 0),
        "input_factor": draw_input_factor(jax.random.fold_in(seeds[4], 71), 0),
    }


def reference(out_grads, activations, output_factor, input_factor):
    grads_grouped = out_grads.reshape(N_DP, TOK_DEV, D_OUT)
    acts_grouped = activations.reshape(N_DP, TOK_DEV, D_IN)

    def add_group(total, pair):
        term = lax.dot_general(pair[0], pair[1], (((0,), (0,)), ((), ())), preferred_element_type=jnp.float32)
        return total + term.astype(jnp.bfloat16).astype(jnp.float32), None

    start = jnp.zeros((D_OUT, D_IN), jnp.float32)
    summed, _ = lax.scan(add_group, start, (grads_grouped, acts_grouped))
    gradient = summed.astype(jnp.bfloat16)
    hidden = jnp.dot(gradient, input_factor, preferred_element_type=jnp.float32).astype(jnp.bfloat16)
    left = output_factor.reshape(D_OUT, D_OUT)
    return jnp.dot(left, hidden, preferred_element_type=jnp.float32).astype(jnp.bfloat16)
```

```python
import functools

import jax
import jax.numpy as jnp
from jax import lax
from jax.experimental import pallas as pl
from jax.experimental.pallas import tpu as pltpu
from jax.sharding import PartitionSpec as P

NX, NY, NZ = 4, 4, 8
BF16, F32 = jnp.bfloat16, jnp.float32
COPIES = 192


def kernel(
    g_hbm, a_hbm, l_hbm, r_hbm, out,
    g_v, a_v, own, give, take, ring_s, ring_r, xs, xr, gt, lbuf, rbuf, r_mine, mbuf, pf, ring2_s, ring2_r,
    load_sem, send_sem, recv_sem, r_send, r_recv,
):
    d, row, y = lax.axis_index("dp"), lax.axis_index("row"), lax.axis_index("col")
    k, z, xh = d % 2, (d // 2) % NZ, d // (2 * NZ)
    x = 2 * xh + row

    def device(x, y, z, k):
        return {"dp": (x // 2) * (2 * NZ) + z * 2 + k, "row": x % 2, "col": y}

    def at_x(n, core=None):
        return device((x + n) % NX, y, z, k if core is None else core)

    def at_y(n):
        return device(x, (y + n) % NY, z, k)

    def at_z(n):
        return device(x, y, (z + n) % NZ, k)

    sibling = device(x, y, z, 1 - k)
    count = [0]
    sent = []

    def send(src, dst, target):
        i = count[0]
        count[0] += 1
        copy = pltpu.make_async_remote_copy(
            src_ref=src, dst_ref=dst, send_sem=send_sem.at[i], recv_sem=recv_sem.at[i],
            device_id=target, device_id_type=pl.DeviceIdType.MESH,
        )
        copy.start()
        sent.append(copy)
        return copy

    loads = []

    def load(src, dst):
        copy = pltpu.make_async_copy(src, dst, load_sem.at[len(loads)])
        copy.start()
        loads.append(copy)
        return copy

    home = z // 4
    load_l = [load(l_hbm.at[0, :, pl.ds(q * 1024, 1024)], lbuf.at[q, z]) for q in range(4)]
    load_r = load(r_hbm, r_mine)
    load_a = load(a_hbm, a_v)
    load_g = load(g_hbm, g_v)

    barrier = pltpu.get_barrier_semaphore()
    partners = [at_z(1), at_z(-1), at_z(4), sibling] + [at_y(n) for n in (1, 2, 3)]
    partners += [at_x(n, core) for n in (1, 2, 3) for core in (k, 1 - k)]
    for partner in partners:
        pl.semaphore_signal(barrier, inc=1, device_id=partner, device_id_type=pl.DeviceIdType.MESH)
    pl.semaphore_wait(barrier, len(partners))

    for copy in load_l:
        copy.wait()
    load_r.wait()

    l_from = {}

    def l_block(q, n):
        return lbuf.at[q, (z + n) % NZ]

    def l_half(q, n, half):
        return lbuf.at[q, (z + n) % NZ, pl.ds(32 * half, 32)]

    def l_z(step):
        if step == 0:
            for sign in (1, -1):
                l_from[sign, 1] = send(l_block(y, 0), l_block(y, 0), at_z(sign))
            return
        for sign in (1, -1):
            l_from[sign, step].wait_recv()
            n = -sign * step
            if step < 3:
                l_from[sign, step + 1] = send(l_block(y, n), l_block(y, n), at_z(sign))
            elif step == 3:
                half = 0 if sign == 1 else 1
                l_from[sign, 4] = send(l_half(y, n, half), l_half(y, n, half), at_z(sign))
        for n in ((-step, step) if step < 4 else (4,)):
            for sign in (1, -1):
                l_from["y", sign, n] = send(l_block(y, n), l_block(y, n), at_y(sign))

    def l_y(*offsets):
        for n in offsets:
            for sign in (1, -1):
                l_from["y", sign, n].wait_recv()
                half = 0 if sign == 1 else 1
                block = l_half((y + NY - sign) % NY, n, half)
                l_from["f", sign, n] = send(block, block, at_y(sign))

    def r_copy(src, dst, i, target):
        return pltpu.make_async_remote_copy(
            src_ref=src, dst_ref=dst, send_sem=r_send.at[i], recv_sem=r_recv.at[i],
            device_id=target, device_id_type=pl.DeviceIdType.MESH,
        )

    away = r_copy(r_mine, rbuf.at[2 * xh + home, row], 0, at_z(4))

    @pl.when(k != home)
    def _():
        away.start()

    pair = rbuf.at[pl.ds(2 * xh, 2), row]
    spread = [r_copy(pair, pair, 1 + n, at_x(n)) for n in (1, 2, 3)]
    spread += [r_copy(pair, pair, 5 + n, at_x(n, 1 - k)) for n in (0, 1, 2, 3)]

    def r_x():
        @pl.when(k == home)
        def _():
            rbuf[2 * xh + home, row] = r_mine[...]
            away.wait_recv()
            for copy in spread:
                copy.start()

    def r_end():
        @pl.when(k == home)
        def _():
            for copy in spread[:3]:
                copy.wait_recv()
            for copy in spread:
                copy.wait_send()

        @pl.when(k != home)
        def _():
            away.wait_send()
            for copy in spread[3:]:
                copy.wait_recv()

    l_z(0)

    exchange = {}

    def term(q_off):
        q = (z + q_off) % 4
        a_part = a_v[:, pl.ds(pl.multiple_of(q * 256, 256), 256)]

        def part(core, n):
            start = pl.multiple_of(core * 1024 + n * 512, 512)
            return lax.dot_general(
                a_part, g_v[:, pl.ds(start, 512)], (((0,), (0,)), ((), ())), preferred_element_type=F32
            )

        for n in range(2):
            give[q, :, n * 512:(n + 1) * 512] = part(1 - k, n).astype(BF16)
        exchange[q_off] = send(give.at[q], take.at[q], sibling)
        for n in range(2):
            own[q, :, n * 512:(n + 1) * 512] = part(k, n)

    def chip_term(n, h):
        chunk = (z + n) % NZ
        rows = pl.ds(pl.multiple_of((chunk // 4) * 128 + h * 64, 64), 64)
        return own[chunk % 4, rows, :] + take[chunk % 4, rows, :].astype(F32)

    def partial(n, h):
        return pf[(z + n) % NZ, h * 32:(h + 1) * 32, :]

    def ring_step(step, mine, buf_s, buf_r, arrived):
        for h, side in ((0, 0), (1, 1), (1, 0), (0, 1)):
            sign = 1 - 2 * side
            if step == 0 and h != side:
                continue
            total = mine(sign * (4 - step), h)
            if (side, h) in arrived:
                arrived[side, h].wait_recv()
                total = total + buf_r[side, h, step - 1].astype(F32)
            buf_s[side, h, step] = total.astype(BF16)
            arrived[side, h] = send(buf_s.at[side, h, step], buf_r.at[side, h, step], at_z(sign))

    def ring_end(h, mine, buf_r, arrived):
        for side in (0, 1):
            arrived[side, h].wait_recv()
        return mine(0, h) + buf_r[0, h, 3].astype(F32) + buf_r[1, h, 3].astype(F32)

    load_a.wait()
    load_g.wait()
    arrived = {}
    term(0)
    term(3)
    exchange[0].wait_recv()
    ring_step(0, chip_term, ring_s, ring_r, arrived)
    term(1)
    l_z(1)
    exchange[3].wait_recv()
    exchange[1].wait_recv()
    ring_step(1, chip_term, ring_s, ring_r, arrived)
    term(2)
    r_x()
    l_z(2)
    exchange[2].wait_recv()
    ring_step(2, chip_term, ring_s, ring_r, arrived)
    l_z(3)
    ring_step(3, chip_term, ring_s, ring_r, arrived)
    l_y(-1, 1)
    l_z(4)

    other, same = 2 * (1 - row) + k, 2 * row + k
    from_x = {}
    for h in (0, 1):
        xs[h] = ring_end(h, chip_term, ring_r, arrived).astype(BF16)
        for side in (0, 1):
            from_x[side, h] = send(xs.at[h], xr.at[side, h], at_x(1 - 2 * side))
    l_y(-2, 2)
    halves, passed = {}, []
    for h in (0, 1):
        for side in (0, 1):
            from_x[side, h].wait_recv()
        rows = pl.ds(64 * h, 64)
        gt[other, rows, :] = (xr[0, h].astype(F32) + xr[1, h].astype(F32)).astype(BF16)
        for side in (0, 1):
            part = gt.at[other, pl.ds(64 * h + 32 * side, 32)]
            halves[side, h] = send(part, part, at_x(1 - 2 * side))
        passed.append(send(gt.at[other, rows], gt.at[other, rows], sibling))
    l_y(-3, 3)
    l_y(4)
    for h in (0, 1):
        for side in (0, 1):
            halves[side, h].wait_recv()
        rows = pl.ds(64 * h, 64)
        passed.append(send(gt.at[same, rows], gt.at[same, rows], sibling))
    for n in (-1, 1, -2, 2, -3, 3, 4):
        for sign in (1, -1):
            l_from["f", sign, n].wait_recv()
    for copy in passed:
        copy.wait_recv()

    left = jnp.zeros((128, 512), F32)
    for q in range(4):
        left = left + lax.dot_general(
            gt[q], lbuf[q].reshape(512, 1024), (((1,), (1,)), ((), ())), preferred_element_type=F32
        )
    mbuf[y] = left.astype(BF16)
    gathered = [send(mbuf.at[y], mbuf.at[y], at_y(n)) for n in (1, 3, 2)]
    r_end()
    for copy in gathered:
        copy.wait_recv()

    left_all = mbuf[...].reshape(512, 512)
    for n in range(2):
        right = rbuf[:, :, :, n * 512:(n + 1) * 512].reshape(512, 512)
        pf[:, :, n * 512:(n + 1) * 512] = lax.dot_general(
            left_all, right, (((0,), (0,)), ((), ())), preferred_element_type=F32
        ).reshape(8, 64, 512)
    arrived2 = {}
    for step in range(4):
        ring_step(step, partial, ring2_s, ring2_r, arrived2)

    def block(half, n, part=None):
        start = (half * NZ + (z + n) % NZ) * 128 + k * 64
        if part is not None:
            return out.at[pl.ds(pl.multiple_of(start + 32 * part, 32), 32)]
        return out.at[pl.ds(pl.multiple_of(start, 64), 64)]

    for h in (0, 1):
        start = pl.multiple_of((xh * NZ + z) * 128 + k * 64 + h * 32, 32)
        out[pl.ds(start, 32), :] = ring_end(h, partial, ring2_r, arrived2).astype(BF16)

    into, across = {}, []

    def start_block(half):
        for side in (0, 1):
            into[half, side, 1] = send(block(xhs[half], 0), block(xhs[half], 0), at_z(1 - 2 * side))
        across.append(send(block(xhs[half], 0), block(xhs[half], 0), sibling))

    xhs = (xh, 1 - xh)
    opposite = send(block(xh, 0), block(xh, 0), at_x(2))
    start_block(0)
    opposite.wait_recv()
    start_block(1)
    for step in range(1, 5):
        for half in (0, 1):
            for side in (0, 1):
                sign = 1 - 2 * side
                into[half, side, step].wait_recv()
                n = -sign * step
                if step < 3:
                    into[half, side, step + 1] = send(block(xhs[half], n), block(xhs[half], n), at_z(sign))
                elif step == 3:
                    into[half, side, 4] = send(block(xhs[half], n, side), block(xhs[half], n, side), at_z(sign))
                if step < 4:
                    across.append(send(block(xhs[half], n), block(xhs[half], n), sibling))
            if step == 4:
                across.append(send(block(xhs[half], 4), block(xhs[half], 4), sibling))
    for copy in across:
        copy.wait_recv()
    for copy in sent:
        copy.wait_send()
    assert count[0] <= COPIES, count[0]


def shards(out_grads, activations, output_factor, input_factor):
    vmem = pltpu.VMEM
    dma = pltpu.SemaphoreType.DMA
    anywhere = pl.BlockSpec(memory_space=pl.ANY)
    return pl.pallas_call(
        kernel,
        out_shape=jax.ShapeDtypeStruct((2048, 1024), BF16),
        in_specs=[anywhere] * 4,
        out_specs=pl.BlockSpec(memory_space=pltpu.VMEM),
        scratch_shapes=[
            vmem((1280, 2048), BF16),
            vmem((1280, 1024), BF16),
            vmem((4, 256, 1024), F32),
            vmem((4, 256, 1024), BF16),
            vmem((4, 256, 1024), BF16),
            vmem((2, 2, 4, 64, 1024), BF16),
            vmem((2, 2, 4, 64, 1024), BF16),
            vmem((2, 64, 1024), BF16),
            vmem((2, 2, 64, 1024), BF16),
            vmem((4, 128, 1024), BF16),
            vmem((4, 8, 64, 1024), BF16),
            vmem((4, 2, 64, 1024), BF16),
            vmem((64, 1024), BF16),
            vmem((4, 128, 512), BF16),
            vmem((8, 64, 1024), F32),
            vmem((2, 2, 4, 32, 1024), BF16),
            vmem((2, 2, 4, 32, 1024), BF16),
            dma((8,)), dma((COPIES,)), dma((COPIES,)), dma((9,)), dma((9,)),
        ],
        compiler_params=pltpu.CompilerParams(
            collective_id=0, has_side_effects=True, vmem_limit_bytes=56 * 2**20
        ),
    )(out_grads, activations, output_factor, input_factor.T)


def solution(mesh):
    placed = (P("dp", "row"), P("dp", "col"), P("row", "dp", None), P("col", ("dp", "row")))
    return jax.shard_map(
        shards, mesh=mesh, in_specs=placed, out_specs=P("row", "col"), check_vma=False
    )
```

```python
import functools

import jax
import jax.numpy as jnp
from jax import lax
from jax.experimental import pallas as pl
from jax.experimental.pallas import tpu as pltpu
from jax.sharding import PartitionSpec as P

NX, NY, NZ = 4, 4, 8
BF16, F32 = jnp.bfloat16, jnp.float32
COPIES = 192


def kernel(
    g_hbm, a_hbm, l_hbm, r_hbm, out,
    g_v, a_v, own, give, take, ring_s, ring_r, xs, xr, gt, lbuf, rbuf, r_mine, mbuf, pf, ring2_s, ring2_r, final,
    load_sem, send_sem, recv_sem, r_send, r_recv,
):
    d, row, y = lax.axis_index("dp"), lax.axis_index("row"), lax.axis_index("col")
    k, z, xh = d % 2, (d // 2) % NZ, d // (2 * NZ)
    x = 2 * xh + row

    def device(x, y, z, k):
        return {"dp": (x // 2) * (2 * NZ) + z * 2 + k, "row": x % 2, "col": y}

    def at_x(n, core=None):
        return device((x + n) % NX, y, z, k if core is None else core)

    def at_y(n):
        return device(x, (y + n) % NY, z, k)

    def at_z(n):
        return device(x, y, (z + n) % NZ, k)

    sibling = device(x, y, z, 1 - k)
    count = [0]
    sent = []

    def send(src, dst, target):
        i = count[0]
        count[0] += 1
        copy = pltpu.make_async_remote_copy(
            src_ref=src, dst_ref=dst, send_sem=send_sem.at[i], recv_sem=recv_sem.at[i],
            device_id=target, device_id_type=pl.DeviceIdType.MESH,
        )
        copy.start()
        sent.append(copy)
        return copy

    loads = []

    def load(src, dst):
        copy = pltpu.make_async_copy(src, dst, load_sem.at[len(loads)])
        copy.start()
        loads.append(copy)
        return copy

    home = z // 4
    load_a = load(a_hbm, a_v)
    load_g = []
    for n in range(4):
        part = pl.ds(pl.multiple_of((n // 2 + (1 - k)) % 2 * 1024 + n % 2 * 512, 512), 512)
        load_g.append(load(g_hbm.at[:, part], g_v.at[:, part]))
    load_l = [load(l_hbm.at[0, :, pl.ds(q * 1024, 1024)], lbuf.at[q, z]) for q in range(4)]
    load_r = load(r_hbm, r_mine)

    barrier = pltpu.get_barrier_semaphore()
    partners = [at_z(1), at_z(-1), at_z(4), sibling] + [at_y(n) for n in (1, 2, 3)]
    partners += [at_x(n, core) for n in (1, 2, 3) for core in (k, 1 - k)]
    for partner in partners:
        pl.semaphore_signal(barrier, inc=1, device_id=partner, device_id_type=pl.DeviceIdType.MESH)

    l_from = {}

    def l_block(q, n):
        return lbuf.at[q, (z + n) % NZ]

    def l_half(q, n, half):
        return lbuf.at[q, (z + n) % NZ, pl.ds(32 * half, 32)]

    def l_z(step):
        if step == 0:
            for sign in (1, -1):
                l_from[sign, 1] = send(l_block(y, 0), l_block(y, 0), at_z(sign))
            return
        for sign in (1, -1):
            n = -sign * step
            if step < 3:
                l_from[sign, step + 1] = send(l_block(y, n), l_block(y, n), at_z(sign))
            elif step == 3:
                half = 0 if sign == 1 else 1
                l_from[sign, 4] = send(l_half(y, n, half), l_half(y, n, half), at_z(sign))

    def l_over_y(step):
        for sign in (1, -1):
            l_from[sign, step].wait_recv()
        for n in ((-step, step) if step < 4 else (4,)):
            for sign in ((1, -1) if step < 3 else (1, -1, 2)):
                l_from["y", sign, n] = send(l_block(y, n), l_block(y, n), at_y(sign))

    def l_y(*offsets):
        for n in offsets:
            for sign in (1, -1):
                l_from["y", sign, n].wait_recv()
                half = 0 if sign == 1 else 1
                block = l_half((y + NY - sign) % NY, n, half)
                l_from["f", sign, n] = send(block, block, at_y(sign))

    def r_copy(src, dst, i, target):
        return pltpu.make_async_remote_copy(
            src_ref=src, dst_ref=dst, send_sem=r_send.at[i], recv_sem=r_recv.at[i],
            device_id=target, device_id_type=pl.DeviceIdType.MESH,
        )

    away = r_copy(r_mine, rbuf.at[2 * xh + home, row], 0, at_z(4))

    pair = rbuf.at[pl.ds(2 * xh, 2), row]
    spread = [r_copy(pair, pair, 1 + n, at_x(n)) for n in (1, 2, 3)]
    spread += [r_copy(pair, pair, 5 + n, at_x(n, 1 - k)) for n in (0, 1, 2, 3)]

    def r_x():
        @pl.when(k == home)
        def _():
            rbuf[2 * xh + home, row] = r_mine[...]
            away.wait_recv()
            for copy in spread:
                copy.start()

    def r_end():
        @pl.when(k == home)
        def _():
            for copy in spread[:3]:
                copy.wait_recv()
            for copy in spread:
                copy.wait_send()

        @pl.when(k != home)
        def _():
            away.wait_send()
            for copy in spread[3:]:
                copy.wait_recv()

    exchange = {}

    def term(q_off, core):
        q = (z + q_off) % 4
        a_part = a_v[:, pl.ds(pl.multiple_of(q * 256, 256), 256)]

        def part(half, n):
            start = pl.multiple_of(half * 1024 + n * 512, 512)
            return lax.dot_general(
                a_part, g_v[:, pl.ds(start, 512)], (((0,), (0,)), ((), ())), preferred_element_type=F32
            )

        if core == 0:
            for n in range(2):
                give[q, :, n * 512:(n + 1) * 512] = part(1 - k, n).astype(BF16)
        else:
            for n in range(2):
                own[q, :, n * 512:(n + 1) * 512] = part(k, n)

    def trade(q_off):
        q = (z + q_off) % 4
        exchange[q_off] = send(give.at[q], take.at[q], sibling)

    def chip_term(n, h):
        chunk = (z + n) % NZ
        rows = pl.ds(pl.multiple_of((chunk // 4) * 128 + h * 64, 64), 64)
        return own[chunk % 4, rows, :] + take[chunk % 4, rows, :].astype(F32)

    def partial(n, h):
        return pf[(z + n) % NZ, h * 32:(h + 1) * 32, :]

    def ring_step(step, mine, buf_s, buf_r, arrived):
        for h, side in ((0, 0), (1, 1), (1, 0), (0, 1)):
            sign = 1 - 2 * side
            if step == 0 and h != side:
                continue
            total = mine(sign * (4 - step), h)
            if (side, h) in arrived:
                arrived[side, h].wait_recv()
                total = total + buf_r[side, h, step - 1].astype(F32)
            buf_s[side, h, step] = total.astype(BF16)
            arrived[side, h] = send(buf_s.at[side, h, step], buf_r.at[side, h, step], at_z(sign))

    def ring_end(h, mine, buf_r, arrived):
        for side in (0, 1):
            arrived[side, h].wait_recv()
        return mine(0, h) + buf_r[0, h, 3].astype(F32) + buf_r[1, h, 3].astype(F32)

    arrived = {}
    load_a.wait()
    for copy in load_g[:2]:
        copy.wait()
    term(0, 0)
    for copy in load_l:
        copy.wait()
    load_r.wait()
    pl.semaphore_wait(barrier, len(partners))
    trade(0)
    l_z(0)

    @pl.when(k != home)
    def _():
        away.start()

    for copy in load_g[2:]:
        copy.wait()
    term(0, 1)
    term(3, 0)
    trade(3)
    exchange[0].wait_recv()
    ring_step(0, chip_term, ring_s, ring_r, arrived)
    term(1, 0)
    trade(1)
    term(3, 1)
    term(1, 1)
    l_over_y(1)
    l_z(1)
    exchange[3].wait_recv()
    exchange[1].wait_recv()
    ring_step(1, chip_term, ring_s, ring_r, arrived)
    term(2, 0)
    trade(2)
    term(2, 1)
    r_x()
    l_over_y(2)
    exchange[2].wait_recv()
    ring_step(2, chip_term, ring_s, ring_r, arrived)
    l_z(2)
    l_y(-1, 1)
    ring_step(3, chip_term, ring_s, ring_r, arrived)
    l_over_y(3)
    l_z(3)

    other, same = 2 * (1 - row) + k, 2 * row + k
    from_x = {}
    for h in (0, 1):
        xs[h] = ring_end(h, chip_term, ring_r, arrived).astype(BF16)
        for side in (0, 1):
            from_x[side, h] = send(xs.at[h], xr.at[side, h], at_x(1 - 2 * side))
    l_y(-2, 2)
    l_over_y(4)
    halves, passed = {}, []
    for h in (0, 1):
        for side in (0, 1):
            from_x[side, h].wait_recv()
        rows = pl.ds(64 * h, 64)
        gt[other, rows, :] = (xr[0, h].astype(F32) + xr[1, h].astype(F32)).astype(BF16)
        for side in (0, 1):
            part = gt.at[other, pl.ds(64 * h + 32 * side, 32)]
            halves[side, h] = send(part, part, at_x(1 - 2 * side))
        passed.append(send(gt.at[other, rows], gt.at[other, rows], sibling))
    for h in (0, 1):
        for side in (0, 1):
            halves[side, h].wait_recv()
        rows = pl.ds(64 * h, 64)
        passed.append(send(gt.at[same, rows], gt.at[same, rows], sibling))
    for n in (-1, 1, -2, 2):
        for sign in (1, -1):
            l_from["f", sign, n].wait_recv()
    for n in (-3, 3, 4):
        for sign in (1, -1, 2):
            l_from["y", sign, n].wait_recv()
    for copy in passed:
        copy.wait_recv()

    left = jnp.zeros((128, 512), F32)
    for q in range(4):
        left = left + lax.dot_general(
            gt[q], lbuf[q].reshape(512, 1024), (((1,), (1,)), ((), ())), preferred_element_type=F32
        )
    mbuf[y] = left.astype(BF16)
    gathered = [send(mbuf.at[y], mbuf.at[y], at_y(n)) for n in (1, 3, 2)]
    r_end()
    for copy in gathered:
        copy.wait_recv()

    left_all = mbuf[...].reshape(512, 512)
    for n in range(2):
        right = rbuf[:, :, :, n * 512:(n + 1) * 512].reshape(512, 512)
        pf[:, :, n * 512:(n + 1) * 512] = lax.dot_general(
            left_all, right, (((0,), (0,)), ((), ())), preferred_element_type=F32
        ).reshape(8, 64, 512)
    arrived2 = {}
    for step in range(4):
        ring_step(step, partial, ring2_s, ring2_r, arrived2)

    def block(half, n, part=None):
        start = (half * NZ + (z + n) % NZ) * 128 + k * 64
        if part is not None:
            return out.at[pl.ds(pl.multiple_of(start + 32 * part, 32), 32)]
        return out.at[pl.ds(pl.multiple_of(start, 64), 64)]

    for h in (0, 1):
        final[h * 32:(h + 1) * 32, :] = ring_end(h, partial, ring2_r, arrived2).astype(BF16)
    place = load(final, block(xh, 0))

    into, across = {}, []

    def start_block(half, src):
        for side in (0, 1):
            into[half, side, 1] = send(src, block(xhs[half], 0), at_z(1 - 2 * side))
        across.append(send(src, block(xhs[half], 0), sibling))

    xhs = (xh, 1 - xh)
    opposite = send(final, block(xh, 0), at_x(2))
    start_block(0, final)
    opposite.wait_recv()
    start_block(1, block(1 - xh, 0))
    for step in range(1, 5):
        for half in (0, 1):
            for side in (0, 1):
                sign = 1 - 2 * side
                into[half, side, step].wait_recv()
                n = -sign * step
                if step < 3:
                    into[half, side, step + 1] = send(block(xhs[half], n), block(xhs[half], n), at_z(sign))
                elif step == 3:
                    into[half, side, 4] = send(block(xhs[half], n, side), block(xhs[half], n, side), at_z(sign))
                if step < 4:
                    across.append(send(block(xhs[half], n), block(xhs[half], n), sibling))
            if step == 4:
                across.append(send(block(xhs[half], 4), block(xhs[half], 4), sibling))
    place.wait()
    for copy in across:
        copy.wait_recv()
    for copy in sent:
        copy.wait_send()
    assert count[0] <= COPIES, count[0]


def shards(out_grads, activations, output_factor, input_factor):
    vmem = pltpu.VMEM
    args = (out_grads, activations, output_factor, input_factor.T)
    dma = pltpu.SemaphoreType.DMA
    anywhere = pl.BlockSpec(memory_space=pl.ANY)
    hbm = pl.BlockSpec(memory_space=pltpu.HBM)
    return pl.pallas_call(
        kernel,
        out_shape=pltpu.VMEM((2048, 1024), BF16),
        in_specs=[hbm] * 4,
        out_specs=anywhere,
        scratch_shapes=[
            vmem((1280, 2048), BF16),
            vmem((1280, 1024), BF16),
            vmem((4, 256, 1024), F32),
            vmem((4, 256, 1024), BF16),
            vmem((4, 256, 1024), BF16),
            vmem((2, 2, 4, 64, 1024), BF16),
            vmem((2, 2, 4, 64, 1024), BF16),
            vmem((2, 64, 1024), BF16),
            vmem((2, 2, 64, 1024), BF16),
            vmem((4, 128, 1024), BF16),
            vmem((4, 8, 64, 1024), BF16),
            vmem((4, 2, 64, 1024), BF16),
            vmem((64, 1024), BF16),
            vmem((4, 128, 512), BF16),
            vmem((8, 64, 1024), F32),
            vmem((2, 2, 4, 32, 1024), BF16),
            vmem((2, 2, 4, 32, 1024), BF16),
            vmem((64, 1024), BF16),
            dma((16,)), dma((COPIES,)), dma((COPIES,)), dma((9,)), dma((9,)),
        ],
        compiler_params=pltpu.CompilerParams(
            collective_id=0, has_side_effects=True, vmem_limit_bytes=40 * 2**20
        ),
    )(*(pltpu.with_memory_space_constraint(v, pltpu.HBM) for v in args))


def solution(mesh):
    placed = (P("dp", "row"), P("dp", "col"), P("row", "dp", None), P("col", ("dp", "row")))
    return jax.shard_map(
        shards, mesh=mesh, in_specs=placed, out_specs=P("row", "col"), check_vma=False
    )
```

```python
import functools

import jax
import jax.numpy as jnp
from jax import lax
from jax.experimental import pallas as pl
from jax.experimental.pallas import tpu as pltpu
from jax.sharding import PartitionSpec as P

NX, NY, NZ = 4, 4, 8
BF16, F32 = jnp.bfloat16, jnp.float32
COPIES = 256


def kernel(
    g_hbm, a_hbm, l_hbm, r_hbm, out,
    g_v, a_v, own, give, take, cross_s, cross_r, ring_s, ring_r, gt, lbuf, rbuf, r_mine, mbuf, pf, far_s, far_r, ring2_s, ring2_r, final,
    load_sem, send_sem, recv_sem, r_send, r_recv,
):
    d, row, y = lax.axis_index("dp"), lax.axis_index("row"), lax.axis_index("col")
    k, z, xh = d % 2, (d // 2) % NZ, d // (2 * NZ)
    x = 2 * xh + row

    def device(x, y, z, k):
        return {"dp": (x // 2) * (2 * NZ) + z * 2 + k, "row": x % 2, "col": y}

    def at_x(n, core=None):
        return device((x + n) % NX, y, z, k if core is None else core)

    def at_y(n):
        return device(x, (y + n) % NY, z, k)

    def at_z(n):
        return device(x, y, (z + n) % NZ, k)

    sibling = device(x, y, z, 1 - k)
    count = [0]
    sent = []

    def send(src, dst, target):
        i = count[0]
        count[0] += 1
        copy = pltpu.make_async_remote_copy(
            src_ref=src, dst_ref=dst, send_sem=send_sem.at[i], recv_sem=recv_sem.at[i],
            device_id=target, device_id_type=pl.DeviceIdType.MESH,
        )
        copy.start()
        sent.append(copy)
        return copy

    loads = []

    def load(src, dst):
        copy = pltpu.make_async_copy(src, dst, load_sem.at[len(loads)])
        copy.start()
        loads.append(copy)
        return copy

    home = z // 4
    load_a = load(a_hbm, a_v)
    load_g = []
    for n in range(4):
        part = pl.ds(pl.multiple_of((n // 2 + (1 - k)) % 2 * 1024 + n % 2 * 512, 512), 512)
        load_g.append(load(g_hbm.at[:, part], g_v.at[:, part]))
    load_l = [load(l_hbm.at[0, :, pl.ds(q * 1024, 1024)], lbuf.at[q, z]) for q in range(4)]
    load_r = load(r_hbm, r_mine)

    barrier = pltpu.get_barrier_semaphore()
    partners = [at_z(1), at_z(-1), at_z(2), at_z(-2), at_z(4), sibling] + [at_y(n) for n in (1, 2, 3)]
    partners += [at_x(n, core) for n in (1, 2, 3) for core in (k, 1 - k)]
    for partner in partners:
        pl.semaphore_signal(barrier, inc=1, device_id=partner, device_id_type=pl.DeviceIdType.MESH)

    l_from = {}

    def l_block(q, n):
        return lbuf.at[q, (z + n) % NZ]

    def l_half(q, n, half):
        return lbuf.at[q, (z + n) % NZ, pl.ds(32 * half, 32)]

    def l_z(step):
        if step == 0:
            for sign in (1, -1):
                l_from[sign, 1] = send(l_block(y, 0), l_block(y, 0), at_z(sign))
            return
        for sign in (1, -1):
            n = -sign * step
            if step < 3:
                l_from[sign, step + 1] = send(l_block(y, n), l_block(y, n), at_z(sign))
            elif step == 3:
                half = 0 if sign == 1 else 1
                l_from[sign, 4] = send(l_half(y, n, half), l_half(y, n, half), at_z(sign))

    def l_over_y(step):
        for sign in (1, -1):
            l_from[sign, step].wait_recv()
        for n in ((-step, step) if step < 4 else (4,)):
            for sign in ((1, -1) if step < 4 else (1, -1, 2)):
                l_from["y", sign, n] = send(l_block(y, n), l_block(y, n), at_y(sign))

    def l_y(*offsets):
        for n in offsets:
            for sign in (1, -1):
                l_from["y", sign, n].wait_recv()
                half = 0 if sign == 1 else 1
                block = l_half((y + NY - sign) % NY, n, half)
                l_from["f", sign, n] = send(block, block, at_y(sign))

    def r_copy(src, dst, i, target):
        return pltpu.make_async_remote_copy(
            src_ref=src, dst_ref=dst, send_sem=r_send.at[i], recv_sem=r_recv.at[i],
            device_id=target, device_id_type=pl.DeviceIdType.MESH,
        )

    away = r_copy(r_mine, rbuf.at[2 * xh + home, row], 0, at_z(4))

    def pair(n):
        source = (x + NX - n) % NX
        return rbuf.at[pl.ds(source // 2 * 2, 2), source % 2]

    spread = [r_copy(pair(0), pair(0), n, at_x(n)) for n in (1, 2, 3)]
    handed = [r_copy(pair(n), pair(n), 4 + n, sibling) for n in range(4)]

    def r_x():
        @pl.when(k == home)
        def _():
            rbuf[2 * xh + home, row] = r_mine[...]
            away.wait_recv()
            for copy in spread:
                copy.start()
            handed[0].start()

    def r_core():
        @pl.when(k == home)
        def _():
            for n in (1, 2, 3):
                spread[n - 1].wait_recv()
                handed[n].start()

    def r_end():
        @pl.when(k == home)
        def _():
            for copy in spread + handed:
                copy.wait_send()

        @pl.when(k != home)
        def _():
            away.wait_send()
            for copy in handed:
                copy.wait_recv()

    exchange = {}

    def term(q_off, core):
        q = (z + q_off) % 4
        a_part = a_v[:, pl.ds(pl.multiple_of(q * 256, 256), 256)]

        def part(half, n):
            start = pl.multiple_of(half * 1024 + n * 512, 512)
            return lax.dot_general(
                a_part, g_v[:, pl.ds(start, 512)], (((0,), (0,)), ((), ())), preferred_element_type=F32
            )

        if core == 0:
            for n in range(2):
                give[q, :, n * 512:(n + 1) * 512] = part(1 - k, n).astype(BF16)
        else:
            for n in range(2):
                own[q, :, n * 512:(n + 1) * 512] = part(k, n)

    def trade(q_off):
        q = (z + q_off) % 4
        exchange[q_off] = send(give.at[q], take.at[q], sibling)

    cross = {}

    def chip_term(n, first, rows):
        chunk = (z + n) % NZ
        rows = pl.ds(pl.multiple_of((chunk // 4) * 128 + first, rows), rows)
        return own[chunk % 4, rows, :] + take[chunk % 4, rows, :].astype(F32)

    def cross_out(*offsets):
        for n in offsets:
            cross_s[n % NZ] = chip_term(n, (1 - xh) * 64, 64).astype(BF16)
            cross[n % NZ] = send(cross_s.at[n % NZ], cross_r.at[n % NZ], at_x(2))

    def half_term(n, h):
        return chip_term(n, xh * 64 + h * 32, 32) + cross_r[n % NZ, h * 32:(h + 1) * 32, :].astype(F32)

    def partial(n, h):
        return pf[h, (z + n) % NZ]

    arrived = {}

    def ring_step(step):
        for sign in (1, -1)[:1 if step == 0 else 2]:
            cross[sign * (4 - step) % NZ].wait_recv()
        for h, side in ((0, 0), (1, 1), (1, 0), (0, 1)):
            sign = 1 - 2 * side
            if step == 0 and h != side:
                continue
            total = half_term(sign * (4 - step), h)
            if (side, h) in arrived:
                arrived[side, h].wait_recv()
                total = total + ring_r[side, h, step - 1].astype(F32)
            ring_s[side, h, step] = total.astype(BF16)
            arrived[side, h] = send(ring_s.at[side, h, step], ring_r.at[side, h, step], at_z(sign))

    load_a.wait()
    for copy in load_g[:2]:
        copy.wait()
    term(0, 0)
    for copy in load_g[2:]:
        copy.wait()
    term(0, 1)
    term(3, 0)
    for copy in load_l:
        copy.wait()
    load_r.wait()
    pl.semaphore_wait(barrier, len(partners))
    trade(0)
    l_z(0)
    trade(3)

    @pl.when(k != home)
    def _():
        away.start()

    exchange[0].wait_recv()
    cross_out(4)
    term(1, 0)
    trade(1)
    term(3, 1)
    exchange[3].wait_recv()
    cross_out(3)
    term(1, 1)
    exchange[1].wait_recv()
    cross_out(-3)
    l_over_y(1)
    l_z(1)
    term(2, 0)
    trade(2)
    ring_step(0)
    term(2, 1)
    exchange[2].wait_recv()
    cross_out(2, -2, 1, -1, 0)
    l_over_y(2)
    l_z(2)
    ring_step(1)
    l_y(-1, 1)
    ring_step(2)
    l_over_y(3)
    l_z(3)
    ring_step(3)
    r_x()
    l_y(-2, 2)
    l_over_y(4)

    def piece_of(n):
        source = (x + NX - n) % NX
        return gt.at[2 * (source % 2) + k, pl.ds(pl.multiple_of(source // 2 * 64, 64), 64)]

    cross[0].wait_recv()
    for h in (0, 1):
        for side in (0, 1):
            arrived[side, h].wait_recv()
        rows = pl.ds(pl.multiple_of(xh * 64 + h * 32, 32), 32)
        gt[2 * row + k, rows, :] = (
            half_term(0, h) + ring_r[0, h, 3].astype(F32) + ring_r[1, h, 3].astype(F32)
        ).astype(BF16)
    from_x = {n: send(piece_of(0), piece_of(0), at_x(n)) for n in (1, 3, 2)}
    passed = [send(piece_of(0), piece_of(0), sibling)]
    l_y(-3, 3)
    for n in (1, 3, 2):
        from_x[n].wait_recv()
        passed.append(send(piece_of(n), piece_of(n), sibling))
    r_core()
    for n in (-1, 1, -2, 2, -3, 3):
        for sign in (1, -1):
            l_from["f", sign, n].wait_recv()
    for sign in (1, -1, 2):
        l_from["y", sign, 4].wait_recv()
    for copy in passed:
        copy.wait_recv()

    gathered = {}
    for h in (0, 1):
        left = jnp.zeros((128, 256), F32)
        for q in range(4):
            left = left + lax.dot_general(
                gt[q], lbuf[q, :, h * 32:(h + 1) * 32, :].reshape(256, 1024), (((1,), (1,)), ((), ())),
                preferred_element_type=F32,
            )
        mbuf[h, y] = left.astype(BF16)
        gathered[h] = [send(mbuf.at[h, y], mbuf.at[h, y], at_y(n)) for n in (1, 3, 2)]
    r_end()

    met, far = {}, {}

    def sum_start(h):
        for side in (0, 1):
            sign = 1 - 2 * side
            if h == side:
                far_s[side] = partial(sign * 4, h).astype(BF16)
                far[side] = send(far_s.at[side], far_r.at[side], at_z(2 * sign))
            ring2_s[side, h, 0] = partial(sign * 3, h).astype(BF16)
            met[side, h] = send(ring2_s.at[side, h, 0], ring2_r.at[side, h, 0], at_z(sign))

    def sum_step(step, h):
        for side in (0, 1):
            sign = 1 - 2 * side
            total = partial(sign * (3 - step), h)
            met[side, h].wait_recv()
            total = total + ring2_r[side, h, step - 1].astype(F32)
            if step == 1 and h == side:
                far[side].wait_recv()
                total = total + far_r[side].astype(F32)
            ring2_s[side, h, step] = total.astype(BF16)
            met[side, h] = send(ring2_s.at[side, h, step], ring2_r.at[side, h, step], at_z(sign))

    for h in (0, 1):
        for copy in gathered[h]:
            copy.wait_recv()
        left_all = mbuf[h].reshape(512, 256)
        for n in range(2):
            right = rbuf[:, :, :, n * 512:(n + 1) * 512].reshape(512, 512)
            pf[h, :, :, n * 512:(n + 1) * 512] = lax.dot_general(
                left_all, right, (((0,), (0,)), ((), ())), preferred_element_type=F32
            ).reshape(8, 32, 512)
        sum_start(h)
    for step in (1, 2):
        for h in (0, 1):
            sum_step(step, h)

    def block(half, n, first=0, rows=64):
        start = (half * NZ + (z + n) % NZ) * 128 + k * 64 + first
        return out.at[pl.ds(pl.multiple_of(start, 16), rows)]

    into, across, crossed = {}, [], {}
    near, away_half = xh, 1 - xh

    def step_out(half, h, side, step):
        sign = 1 - 2 * side
        n = -sign * (step - 1)
        piece = block(half, n, 32 * h, 32)
        into[half is near, h, side, step] = send(piece, piece, at_z(sign))
        if step == 3:
            quarter = block(half, n, 32 * h + 16 * side, 16)
            into[half is near, h, side, 4] = send(quarter, quarter, at_z(2 * sign))

    def over_x(n):
        piece = block(near, n, 32, 32)
        crossed[n] = send(piece, piece, at_x(2))

    def over_core(half, n, first=0, rows=64):
        piece = block(half, n, first, rows)
        across.append(send(piece, piece, sibling))

    for h in (1, 0):
        for side in (0, 1):
            met[side, h].wait_recv()
        rows = slice(h * 32, (h + 1) * 32)
        final[rows, :] = (
            partial(0, h) + ring2_r[0, h, 2].astype(F32) + ring2_r[1, h, 2].astype(F32)
        ).astype(BF16)
        place = load(final.at[pl.ds(h * 32, 32)], block(near, 0, 32 * h, 32))
        place.wait()
        if h == 0:
            crossed["h0"] = send(block(near, 0, 0, 32), block(near, 0, 0, 32), at_x(2))
        for side in (0, 1):
            step_out(near, h, side, 1)
        if h == 1:
            over_x(0)
    over_core(near, 0)

    def own_class(step):
        for h in (1, 0):
            for side in (0, 1):
                into[True, h, side, step].wait_recv()
                if step < 3:
                    step_out(near, h, side, step + 1)
                if h == 1 and step < 4:
                    over_x((2 * side - 1) * step)
            if h == 1 and step == 4:
                over_x(4)
        for n in ((-step, step) if step < 4 else (4,)):
            over_core(near, n)

    def opposite(step):
        for side in (0, 1):
            into[False, 0, side, step].wait_recv()
            if step < 3:
                step_out(away_half, 0, side, step + 1)
        for n in ((-step, step) if step < 4 else (4,)):
            over_core(away_half, n, 0, 32)

    def from_opposite(*offsets):
        for n in offsets:
            crossed[n].wait_recv()
            over_core(away_half, n, 32, 32)

    own_class(1)
    crossed["h0"].wait_recv()
    for side in (0, 1):
        step_out(away_half, 0, side, 1)
    over_core(away_half, 0, 0, 32)
    own_class(2)
    from_opposite(0)
    opposite(1)
    from_opposite(-1, 1)
    own_class(3)
    own_class(4)
    opposite(2)
    from_opposite(-2, 2)
    opposite(3)
    opposite(4)
    from_opposite(-3, 3, 4)
    for copy in across:
        copy.wait_recv()
    for copy in sent:
        copy.wait_send()
    assert count[0] <= COPIES, count[0]


def shards(out_grads, activations, output_factor, input_factor):
    vmem = pltpu.VMEM
    args = (out_grads, activations, output_factor, input_factor.T)
    dma = pltpu.SemaphoreType.DMA
    anywhere = pl.BlockSpec(memory_space=pl.ANY)
    hbm = pl.BlockSpec(memory_space=pltpu.HBM)
    return pl.pallas_call(
        kernel,
        out_shape=pltpu.VMEM((2048, 1024), BF16),
        in_specs=[hbm] * 4,
        out_specs=anywhere,
        scratch_shapes=[
            vmem((1280, 2048), BF16),
            vmem((1280, 1024), BF16),
            vmem((4, 256, 1024), F32),
            vmem((4, 256, 1024), BF16),
            vmem((4, 256, 1024), BF16),
            vmem((8, 64, 1024), BF16),
            vmem((8, 64, 1024), BF16),
            vmem((2, 2, 4, 32, 1024), BF16),
            vmem((2, 2, 4, 32, 1024), BF16),
            vmem((4, 128, 1024), BF16),
            vmem((4, 8, 64, 1024), BF16),
            vmem((4, 2, 64, 1024), BF16),
            vmem((64, 1024), BF16),
            vmem((2, 4, 128, 256), BF16),
            vmem((2, 8, 32, 1024), F32),
            vmem((2, 32, 1024), BF16),
            vmem((2, 32, 1024), BF16),
            vmem((2, 2, 3, 32, 1024), BF16),
            vmem((2, 2, 3, 32, 1024), BF16),
            vmem((64, 1024), BF16),
            dma((16,)), dma((COPIES,)), dma((COPIES,)), dma((9,)), dma((9,)),
        ],
        compiler_params=pltpu.CompilerParams(
            collective_id=0, has_side_effects=True, vmem_limit_bytes=40 * 2**20
        ),
    )(*(pltpu.with_memory_space_constraint(v, pltpu.HBM) for v in args))


def solution(mesh):
    placed = (P("dp", "row"), P("dp", "col"), P("row", "dp", None), P("col", ("dp", "row")))
    return jax.shard_map(
        shards, mesh=mesh, in_specs=placed, out_specs=P("row", "col"), check_vma=False
    )
```

```python
import functools

import jax
import jax.numpy as jnp
from jax import lax
from jax.experimental import pallas as pl
from jax.experimental.pallas import tpu as pltpu
from jax.sharding import PartitionSpec as P

NX, NY, NZ = 4, 4, 8
BF16, F32 = jnp.bfloat16, jnp.float32
COPIES = 146


def kernel(
    g_hbm, a_hbm, l_hbm, r_hbm, out,
    g_v, a_v, own, give, take, cross_s, cross_r, ring_s, ring_r, gt, lbuf, rbuf, r_mine, mbuf, pf, far_s, far_r, ring2_s, ring2_r, final,
    load_sem, send_sem, recv_sem, r_send, r_recv,
):
    d, row, y = lax.axis_index("dp"), lax.axis_index("row"), lax.axis_index("col")
    k, z, xh = d % 2, (d // 2) % NZ, d // (2 * NZ)
    x = 2 * xh + row

    def device(x, y, z, k):
        return {"dp": (x // 2) * (2 * NZ) + z * 2 + k, "row": x % 2, "col": y}

    def at_x(n, core=None):
        return device((x + n) % NX, y, z, k if core is None else core)

    def at_y(n):
        return device(x, (y + n) % NY, z, k)

    def at_z(n):
        return device(x, y, (z + n) % NZ, k)

    sibling = device(x, y, z, 1 - k)
    count = [0]
    sent = []

    def send(src, dst, target):
        i = count[0]
        count[0] += 1
        copy = pltpu.make_async_remote_copy(
            src_ref=src, dst_ref=dst, send_sem=send_sem.at[i], recv_sem=recv_sem.at[i],
            device_id=target, device_id_type=pl.DeviceIdType.MESH,
        )
        copy.start()
        sent.append(copy)
        return copy

    def retire(count):
        for copy in sent[:count]:
            copy.wait_send()
        del sent[:count]

    loads = []

    def load(src, dst):
        copy = pltpu.make_async_copy(src, dst, load_sem.at[len(loads)])
        copy.start()
        loads.append(copy)
        return copy

    home = z // 4
    load_a, load_g = {}, []

    def load_columns(n):
        part = pl.ds(pl.multiple_of((z + n) % 4 * 256, 256), 256)
        load_a[n] = load(a_hbm.at[:, part], a_v.at[:, part])

    load_columns(0)
    for n in range(4):
        part = pl.ds(pl.multiple_of((n // 2 + (1 - k)) % 2 * 1024 + n % 2 * 512, 512), 512)
        load_g.append(load(g_hbm.at[:, part], g_v.at[:, part]))
    for n in (3, 1, 2):
        load_columns(n)
    load_l = [load(l_hbm.at[0, :, pl.ds(q * 1024, 1024)], lbuf.at[q, z]) for q in range(4)]
    load_r = load(r_hbm, r_mine)

    barrier = pltpu.get_barrier_semaphore()
    partners = [at_z(1), at_z(-1), at_z(2), at_z(-2), at_z(4), sibling] + [at_y(n) for n in (1, 2, 3)]
    partners += [at_x(n, core) for n in (1, 2, 3) for core in (k, 1 - k)]
    for partner in partners:
        pl.semaphore_signal(barrier, inc=1, device_id=partner, device_id_type=pl.DeviceIdType.MESH)

    l_from = {}

    def l_block(q, n):
        return lbuf.at[q, (z + n) % NZ]

    def l_half(q, n, half):
        return lbuf.at[q, (z + n) % NZ, pl.ds(32 * half, 32)]

    def l_z(step):
        if step == 0:
            for sign in (1, -1):
                l_from[sign, 1] = send(l_block(y, 0), l_block(y, 0), at_z(sign))
            return
        for sign in (1, -1):
            n = -sign * step
            if step < 3:
                l_from[sign, step + 1] = send(l_block(y, n), l_block(y, n), at_z(sign))
            elif step == 3:
                half = 0 if sign == 1 else 1
                l_from[sign, 4] = send(l_half(y, n, half), l_half(y, n, half), at_z(sign))

    def l_over_y(step):
        for sign in (1, -1):
            l_from[sign, step].wait_recv()
        for n in ((-step, step) if step < 4 else (4,)):
            for sign in ((1, -1) if step < 4 else (1, -1, 2)):
                l_from["y", sign, n] = send(l_block(y, n), l_block(y, n), at_y(sign))

    def l_y(*offsets):
        for n in offsets:
            for sign in (1, -1):
                l_from["y", sign, n].wait_recv()
                half = 0 if sign == 1 else 1
                block = l_half((y + NY - sign) % NY, n, half)
                l_from["f", sign, n] = send(block, block, at_y(sign))

    def r_copy(src, dst, i, target):
        return pltpu.make_async_remote_copy(
            src_ref=src, dst_ref=dst, send_sem=r_send.at[i], recv_sem=r_recv.at[i],
            device_id=target, device_id_type=pl.DeviceIdType.MESH,
        )

    away = r_copy(r_mine, rbuf.at[2 * xh + home, row], 0, at_z(4))

    def pair(n):
        source = (x + NX - n) % NX
        return rbuf.at[pl.ds(source // 2 * 2, 2), source % 2]

    def slot(source, n):
        return rbuf.at[2 * (source // 2) + n, source % 2]

    own_spread = [r_copy(r_mine, slot(x, home), n, at_x(n)) for n in (1, 2, 3)]
    far_spread = [r_copy(slot(x, 1 - home), slot(x, 1 - home), 3 + n, at_x(n)) for n in (1, 2, 3)]
    handed = [r_copy(pair(n), pair(n), 7 + n, sibling) for n in range(4)]

    def r_first():
        @pl.when(k == home)
        def _():
            for copy in own_spread:
                copy.start()
            rbuf[2 * xh + home, row] = r_mine[...]

    def r_away():
        @pl.when(k != home)
        def _():
            away.start()

    def r_second():
        @pl.when(k == home)
        def _():
            away.wait_recv()
            for copy in far_spread:
                copy.start()
            handed[0].start()

    def r_core():
        @pl.when(k == home)
        def _():
            for n in (1, 2, 3):
                own_spread[n - 1].wait_recv()
                far_spread[n - 1].wait_recv()
                handed[n].start()

    def r_end():
        @pl.when(k == home)
        def _():
            for copy in own_spread + far_spread + handed:
                copy.wait_send()

        @pl.when(k != home)
        def _():
            away.wait_send()
            for copy in handed:
                copy.wait_recv()

    exchange = {}

    def term(q_off, core):
        q = (z + q_off) % 4
        a_part = a_v[:, pl.ds(pl.multiple_of(q * 256, 256), 256)]

        def part(half, n):
            start = pl.multiple_of(half * 1024 + n * 512, 512)
            return lax.dot_general(
                a_part, g_v[:, pl.ds(start, 512)], (((0,), (0,)), ((), ())), preferred_element_type=F32
            )

        if core == 0:
            for n in range(2):
                give[q, :, n * 512:(n + 1) * 512] = part(1 - k, n).astype(BF16)
        else:
            for n in range(2):
                own[q, :, n * 512:(n + 1) * 512] = part(k, n)

    def trade(q_off):
        q = (z + q_off) % 4
        exchange[q_off] = send(give.at[q], take.at[q], sibling)

    cross = {}

    def chip_term(n, first, rows):
        chunk = (z + n) % NZ
        rows = pl.ds(pl.multiple_of((chunk // 4) * 128 + first, rows), rows)
        return own[chunk % 4, rows, :] + take[chunk % 4, rows, :].astype(F32)

    def cross_out(*offsets):
        for n in offsets:
            cross_s[n % NZ] = chip_term(n, (1 - xh) * 64, 64).astype(BF16)
            cross[n % NZ] = send(cross_s.at[n % NZ], cross_r.at[n % NZ], at_x(2))

    def half_term(n, h):
        return chip_term(n, xh * 64 + h * 32, 32) + cross_r[n % NZ, h * 32:(h + 1) * 32, :].astype(F32)

    def partial(n, h):
        return pf[h, (z + n) % NZ]

    arrived = {}

    def ring_step(step):
        for sign in (1, -1)[:1 if step == 0 else 2]:
            cross[sign * (4 - step) % NZ].wait_recv()
        for h, side in ((0, 0), (1, 1), (1, 0), (0, 1)):
            sign = 1 - 2 * side
            if step == 0 and h != side:
                continue
            total = half_term(sign * (4 - step), h)
            if (side, h) in arrived:
                arrived[side, h].wait_recv()
                total = total + ring_r[side, h, step - 1].astype(F32)
            ring_s[side, h, step] = total.astype(BF16)
            arrived[side, h] = send(ring_s.at[side, h, step], ring_r.at[side, h, step], at_z(sign))

    load_a[0].wait()
    for copy in load_g[:2]:
        copy.wait()
    term(0, 0)
    for copy in load_l:
        copy.wait()
    load_r.wait()
    pl.semaphore_wait(barrier, len(partners))
    trade(0)
    l_z(0)
    r_first()
    for copy in load_g[2:]:
        copy.wait()
    term(0, 1)
    load_a[3].wait()
    term(3, 0)
    trade(3)
    exchange[0].wait_recv()
    cross_out(4)
    load_a[1].wait()
    load_a[2].wait()
    term(1, 0)
    trade(1)
    term(3, 1)
    exchange[3].wait_recv()
    cross_out(3)
    term(1, 1)
    exchange[1].wait_recv()
    cross_out(-3)
    l_over_y(1)
    l_z(1)
    term(2, 0)
    trade(2)
    ring_step(0)
    r_away()
    term(2, 1)
    exchange[2].wait_recv()
    cross_out(2, -2, 1, -1, 0)
    l_over_y(2)
    l_z(2)
    ring_step(1)
    l_y(-1, 1)
    retire(12)
    ring_step(2)
    l_over_y(3)
    l_z(3)
    ring_step(3)
    l_y(-2, 2)
    l_over_y(4)
    retire(30)

    def piece_of(n):
        source = (x + NX - n) % NX
        return gt.at[2 * (source % 2) + k, pl.ds(pl.multiple_of(source // 2 * 64, 64), 64)]

    cross[0].wait_recv()
    for h in (0, 1):
        for side in (0, 1):
            arrived[side, h].wait_recv()
        rows = pl.ds(pl.multiple_of(xh * 64 + h * 32, 32), 32)
        gt[2 * row + k, rows, :] = (
            half_term(0, h) + ring_r[0, h, 3].astype(F32) + ring_r[1, h, 3].astype(F32)
        ).astype(BF16)
    from_x = {n: send(piece_of(0), piece_of(0), at_x(n)) for n in (1, 3, 2)}
    passed = [send(piece_of(0), piece_of(0), sibling)]
    l_y(-3, 3)
    for n in (1, 3, 2):
        from_x[n].wait_recv()
        passed.append(send(piece_of(n), piece_of(n), sibling))
    r_second()
    for n in (-1, 1, -2, 2, -3, 3):
        for sign in (1, -1):
            l_from["f", sign, n].wait_recv()
    for sign in (1, -1, 2):
        l_from["y", sign, 4].wait_recv()
    for copy in passed:
        copy.wait_recv()

    gathered = {}
    for h in (0, 1):
        left = jnp.zeros((128, 256), F32)
        for q in range(4):
            left = left + lax.dot_general(
                gt[q], lbuf[q, :, h * 32:(h + 1) * 32, :].reshape(256, 1024), (((1,), (1,)), ((), ())),
                preferred_element_type=F32,
            )
        mbuf[h, y] = left.astype(BF16)
        gathered[h] = [send(mbuf.at[h, y], mbuf.at[h, y], at_y(n)) for n in (1, 3, 2)]
    r_core()
    retire(len(sent) - 10)
    r_end()

    met, far = {}, {}

    def sum_start(h):
        for side in (0, 1):
            sign = 1 - 2 * side
            if h == side:
                far_s[side] = partial(sign * 4, h).astype(BF16)
                far[side] = send(far_s.at[side], far_r.at[side], at_z(2 * sign))
            ring2_s[side, h, 0] = partial(sign * 3, h).astype(BF16)
            met[side, h] = send(ring2_s.at[side, h, 0], ring2_r.at[side, h, 0], at_z(sign))

    def sum_step(step, h):
        for side in (0, 1):
            sign = 1 - 2 * side
            total = partial(sign * (3 - step), h)
            met[side, h].wait_recv()
            total = total + ring2_r[side, h, step - 1].astype(F32)
            if step == 1 and h == side:
                far[side].wait_recv()
                total = total + far_r[side].astype(F32)
            ring2_s[side, h, step] = total.astype(BF16)
            met[side, h] = send(ring2_s.at[side, h, step], ring2_r.at[side, h, step], at_z(sign))

    for h in (0, 1):
        for copy in gathered[h]:
            copy.wait_recv()
        left_all = mbuf[h].reshape(512, 256)
        for n in range(2):
            right = rbuf[:, :, :, n * 512:(n + 1) * 512].reshape(512, 512)
            pf[h, :, :, n * 512:(n + 1) * 512] = lax.dot_general(
                left_all, right, (((0,), (0,)), ((), ())), preferred_element_type=F32
            ).reshape(8, 32, 512)
        sum_start(h)
    for step in (1, 2):
        for h in (0, 1):
            sum_step(step, h)

    def block(half, n, first=0, rows=64):
        start = (half * NZ + (z + n) % NZ) * 128 + k * 64 + first
        return out.at[pl.ds(pl.multiple_of(start, 16), rows)]

    into, across, crossed = {}, [], {}
    near, away_half = xh, 1 - xh

    def step_out(half, h, side, step):
        sign = 1 - 2 * side
        n = -sign * (step - 1)
        piece = block(half, n, 32 * h, 32)
        into[half is near, h, side, step] = send(piece, piece, at_z(sign))
        if step == 3:
            quarter = block(half, n, 32 * h + 16 * side, 16)
            into[half is near, h, side, 4] = send(quarter, quarter, at_z(2 * sign))

    def over_x(n):
        piece = block(near, n, 32, 32)
        crossed[n] = send(piece, piece, at_x(2))

    def over_core(half, n, first=0, rows=64):
        piece = block(half, n, first, rows)
        across.append(send(piece, piece, sibling))

    def mine(h):
        return final.at[pl.ds(h * 32, 32)], block(near, 0, 32 * h, 32)

    places = []
    for h in (0, 1):
        for side in (0, 1):
            met[side, h].wait_recv()
        final[h * 32:(h + 1) * 32, :] = (
            partial(0, h) + ring2_r[0, h, 2].astype(F32) + ring2_r[1, h, 2].astype(F32)
        ).astype(BF16)
        if h == 0:
            crossed["h0"] = send(*mine(0), at_x(2))
        places.append(load(*mine(h)))
    for h in (1, 0):
        for side in (0, 1):
            into[True, h, side, 1] = send(*mine(h), at_z(1 - 2 * side))
        if h == 1:
            crossed[0] = send(*mine(1), at_x(2))
    for h in (0, 1):
        across.append(send(*mine(h), sibling))

    def own_class(step):
        for h in (1, 0):
            for side in (0, 1):
                into[True, h, side, step].wait_recv()
                if step < 3:
                    step_out(near, h, side, step + 1)
                if h == 1 and step < 4:
                    over_x((2 * side - 1) * step)
            if h == 1 and step == 4:
                over_x(4)
        for n in ((-step, step) if step < 4 else (4,)):
            over_core(near, n)

    def opposite(step):
        for side in (0, 1):
            into[False, 0, side, step].wait_recv()
            if step < 3:
                step_out(away_half, 0, side, step + 1)
        for n in ((-step, step) if step < 4 else (4,)):
            over_core(away_half, n, 0, 32)

    def from_opposite(*offsets):
        for n in offsets:
            crossed[n].wait_recv()
            over_core(away_half, n, 32, 32)

    retire(len(sent) - 16)
    own_class(1)
    crossed["h0"].wait_recv()
    for side in (0, 1):
        step_out(away_half, 0, side, 1)
    over_core(away_half, 0, 0, 32)
    own_class(2)
    from_opposite(0)
    opposite(1)
    from_opposite(-1, 1)
    retire(len(sent) - 34)
    own_class(3)
    own_class(4)
    retire(len(sent) - 34)
    opposite(2)
    from_opposite(-2, 2)
    opposite(3)
    opposite(4)
    from_opposite(-3, 3, 4)
    retire(len(sent) - 14)
    for copy in places:
        copy.wait()
    for copy in across:
        copy.wait_recv()
    for copy in sent:
        copy.wait_send()
    assert count[0] == COPIES, count[0]


def shards(out_grads, activations, output_factor, input_factor):
    vmem = pltpu.VMEM
    args = (out_grads, activations, output_factor, input_factor.T)
    dma = pltpu.SemaphoreType.DMA
    anywhere = pl.BlockSpec(memory_space=pl.ANY)
    hbm = pl.BlockSpec(memory_space=pltpu.HBM)
    return pl.pallas_call(
        kernel,
        out_shape=pltpu.VMEM((2048, 1024), BF16),
        in_specs=[hbm] * 4,
        out_specs=anywhere,
        scratch_shapes=[
            vmem((1280, 2048), BF16),
            vmem((1280, 1024), BF16),
            vmem((4, 256, 1024), F32),
            vmem((4, 256, 1024), BF16),
            vmem((4, 256, 1024), BF16),
            vmem((8, 64, 1024), BF16),
            vmem((8, 64, 1024), BF16),
            vmem((2, 2, 4, 32, 1024), BF16),
            vmem((2, 2, 4, 32, 1024), BF16),
            vmem((4, 128, 1024), BF16),
            vmem((4, 8, 64, 1024), BF16),
            vmem((4, 2, 64, 1024), BF16),
            vmem((64, 1024), BF16),
            vmem((2, 4, 128, 256), BF16),
            vmem((2, 8, 32, 1024), F32),
            vmem((2, 32, 1024), BF16),
            vmem((2, 32, 1024), BF16),
            vmem((2, 2, 3, 32, 1024), BF16),
            vmem((2, 2, 3, 32, 1024), BF16),
            vmem((64, 1024), BF16),
            dma((16,)), dma((COPIES,)), dma((COPIES,)), dma((11,)), dma((11,)),
        ],
        compiler_params=pltpu.CompilerParams(
            collective_id=0, has_side_effects=True, vmem_limit_bytes=40 * 2**20
        ),
    )(*(pltpu.with_memory_space_constraint(v, pltpu.HBM) for v in args))


def solution(mesh):
    placed = (P("dp", "row"), P("dp", "col"), P("row", "dp", None), P("col", ("dp", "row")))
    return jax.shard_map(
        shards, mesh=mesh, in_specs=placed, out_specs=P("row", "col"), check_vma=False
    )
```

```python
import functools

import jax
import jax.numpy as jnp
from jax import lax
from jax.experimental import pallas as pl
from jax.experimental.pallas import tpu as pltpu
from jax.sharding import PartitionSpec as P

NX, NY, NZ = 4, 4, 8
BF16, F32 = jnp.bfloat16, jnp.float32
COPIES = 146


def kernel(
    g_hbm, a_hbm, l_hbm, r_hbm, out,
    g_v, a_v, own, give, take, cross_s, cross_r, ring_s, ring_r, gt, lbuf, rbuf, r_mine, mbuf, pf, far_s, far_r, ring2_s, ring2_r, final,
    load_sem, send_sem, recv_sem, r_send, r_recv,
):
    d, row, y = lax.axis_index("dp"), lax.axis_index("row"), lax.axis_index("col")
    k, z, xh = d % 2, (d // 2) % NZ, d // (2 * NZ)
    x = 2 * xh + row

    def device(x, y, z, k):
        return {"dp": (x // 2) * (2 * NZ) + z * 2 + k, "row": x % 2, "col": y}

    def at_x(n, core=None):
        return device((x + n) % NX, y, z, k if core is None else core)

    def at_y(n):
        return device(x, (y + n) % NY, z, k)

    def at_z(n):
        return device(x, y, (z + n) % NZ, k)

    sibling = device(x, y, z, 1 - k)
    count = [0]
    sent = []

    def send(src, dst, target):
        i = count[0]
        count[0] += 1
        copy = pltpu.make_async_remote_copy(
            src_ref=src, dst_ref=dst, send_sem=send_sem.at[i], recv_sem=recv_sem.at[i],
            device_id=target, device_id_type=pl.DeviceIdType.MESH,
        )
        copy.start()
        sent.append(copy)
        return copy

    def retire(count):
        for copy in sent[:count]:
            copy.wait_send()
        del sent[:count]

    loads = []

    def load(src, dst):
        copy = pltpu.make_async_copy(src, dst, load_sem.at[len(loads)])
        copy.start()
        loads.append(copy)
        return copy

    home = z // 4
    load_a, load_g = {}, []

    def load_columns(n):
        part = pl.ds(pl.multiple_of((z + n) % 4 * 256, 256), 256)
        load_a[n] = load(a_hbm.at[:, part], a_v.at[:, part])

    load_columns(0)
    for n in range(4):
        part = pl.ds(pl.multiple_of((n // 2 + (1 - k)) % 2 * 1024 + n % 2 * 512, 512), 512)
        load_g.append(load(g_hbm.at[:, part], g_v.at[:, part]))
    for n in (3, 1, 2):
        load_columns(n)
    load_l = [load(l_hbm.at[0, :, pl.ds(q * 1024, 1024)], lbuf.at[q, z]) for q in range(4)]
    load_r = load(r_hbm, r_mine)

    barrier = pltpu.get_barrier_semaphore()
    partners = [at_z(1), at_z(-1), at_z(2), at_z(-2), at_z(4), sibling] + [at_y(n) for n in (1, 2, 3)]
    partners += [at_x(n, core) for n in (1, 2, 3) for core in (k, 1 - k)]
    for partner in partners:
        pl.semaphore_signal(barrier, inc=1, device_id=partner, device_id_type=pl.DeviceIdType.MESH)

    l_from = {}

    def l_block(q, n):
        return lbuf.at[q, (z + n) % NZ]

    def l_half(q, n, half):
        return lbuf.at[q, (z + n) % NZ, pl.ds(32 * half, 32)]

    def l_z(step):
        if step == 0:
            for sign in (1, -1):
                l_from[sign, 1] = send(l_block(y, 0), l_block(y, 0), at_z(sign))
            return
        for sign in (1, -1):
            n = -sign * step
            if step < 3:
                l_from[sign, step + 1] = send(l_block(y, n), l_block(y, n), at_z(sign))
            elif step == 3:
                half = 0 if sign == 1 else 1
                l_from[sign, 4] = send(l_half(y, n, half), l_half(y, n, half), at_z(sign))

    def l_over_y(step):
        for sign in (1, -1):
            l_from[sign, step].wait_recv()
        for n in ((-step, step) if step < 4 else (4,)):
            for sign in ((1, -1) if step < 4 else (1, -1, 2)):
                l_from["y", sign, n] = send(l_block(y, n), l_block(y, n), at_y(sign))

    def l_y(*offsets):
        for n in offsets:
            for sign in (1, -1):
                l_from["y", sign, n].wait_recv()
                half = 0 if sign == 1 else 1
                block = l_half((y + NY - sign) % NY, n, half)
                l_from["f", sign, n] = send(block, block, at_y(sign))

    def r_copy(src, dst, i, target):
        return pltpu.make_async_remote_copy(
            src_ref=src, dst_ref=dst, send_sem=r_send.at[i], recv_sem=r_recv.at[i],
            device_id=target, device_id_type=pl.DeviceIdType.MESH,
        )

    away = r_copy(r_mine, rbuf.at[2 * xh + home, row], 0, at_z(4))

    def pair(n):
        source = (x + NX - n) % NX
        return rbuf.at[pl.ds(source // 2 * 2, 2), source % 2]

    def slot(source, n):
        return rbuf.at[2 * (source // 2) + n, source % 2]

    own_spread = [r_copy(r_mine, slot(x, home), n, at_x(n)) for n in (1, 2, 3)]
    far_spread = [r_copy(slot(x, 1 - home), slot(x, 1 - home), 3 + n, at_x(n)) for n in (1, 2, 3)]
    handed = [r_copy(pair(n), pair(n), 7 + n, sibling) for n in range(4)]

    def r_first():
        @pl.when(k == home)
        def _():
            for copy in own_spread:
                copy.start()
            rbuf[2 * xh + home, row] = r_mine[...]

    def r_away():
        @pl.when(k != home)
        def _():
            away.start()

    def r_second():
        @pl.when(k == home)
        def _():
            away.wait_recv()
            for copy in far_spread:
                copy.start()
            handed[0].start()

    def r_core():
        @pl.when(k == home)
        def _():
            for n in (1, 2, 3):
                own_spread[n - 1].wait_recv()
                far_spread[n - 1].wait_recv()
                handed[n].start()

    def r_end():
        @pl.when(k == home)
        def _():
            for copy in own_spread + far_spread + handed:
                copy.wait_send()

        @pl.when(k != home)
        def _():
            away.wait_send()
            for copy in handed:
                copy.wait_recv()

    exchange = {}

    def term(q_off, core):
        q = (z + q_off) % 4
        a_part = a_v[:, pl.ds(pl.multiple_of(q * 256, 256), 256)]

        def part(half, n):
            start = pl.multiple_of(half * 1024 + n * 512, 512)
            return lax.dot_general(
                a_part, g_v[:, pl.ds(start, 512)], (((0,), (0,)), ((), ())), preferred_element_type=F32
            )

        if core == 0:
            for n in range(2):
                give[q, :, n * 512:(n + 1) * 512] = part(1 - k, n).astype(BF16)
        else:
            for n in range(2):
                own[q, :, n * 512:(n + 1) * 512] = part(k, n)

    def trade(q_off):
        q = (z + q_off) % 4
        exchange[q_off] = send(give.at[q], take.at[q], sibling)

    cross = {}

    def chip_term(n, first, rows):
        chunk = (z + n) % NZ
        rows = pl.ds(pl.multiple_of((chunk // 4) * 128 + first, rows), rows)
        return own[chunk % 4, rows, :] + take[chunk % 4, rows, :].astype(F32)

    def cross_out(*offsets):
        for n in offsets:
            cross_s[n % NZ] = chip_term(n, (1 - xh) * 64, 64).astype(BF16)
            cross[n % NZ] = send(cross_s.at[n % NZ], cross_r.at[n % NZ], at_x(2))

    def half_term(n, h):
        return chip_term(n, xh * 64 + h * 32, 32) + cross_r[n % NZ, h * 32:(h + 1) * 32, :].astype(F32)

    def partial(n, h):
        return pf[h, (z + n) % NZ]

    arrived = {}

    def ring_step(step):
        for sign in (1, -1)[:1 if step == 0 else 2]:
            cross[sign * (4 - step) % NZ].wait_recv()
        for h, side in ((0, 0), (1, 1), (1, 0), (0, 1)):
            sign = 1 - 2 * side
            if step == 0 and h != side:
                continue
            total = half_term(sign * (4 - step), h)
            if (side, h) in arrived:
                arrived[side, h].wait_recv()
                total = total + ring_r[side, h, step - 1].astype(F32)
            ring_s[side, h, step] = total.astype(BF16)
            arrived[side, h] = send(ring_s.at[side, h, step], ring_r.at[side, h, step], at_z(sign))

    load_a[0].wait()
    for copy in load_g[:2]:
        copy.wait()
    term(0, 0)
    for copy in load_l:
        copy.wait()
    load_r.wait()
    pl.semaphore_wait(barrier, len(partners))
    trade(0)
    l_z(0)
    for copy in load_g[2:]:
        copy.wait()
    term(0, 1)
    load_a[3].wait()
    term(3, 0)
    trade(3)
    exchange[0].wait_recv()
    cross_out(4)
    load_a[1].wait()
    load_a[2].wait()
    term(1, 0)
    trade(1)
    term(3, 1)
    exchange[3].wait_recv()
    cross_out(3)
    term(1, 1)
    exchange[1].wait_recv()
    cross_out(-3)
    l_over_y(1)
    l_z(1)
    term(2, 0)
    trade(2)
    term(2, 1)
    exchange[2].wait_recv()
    cross_out(2, -2)
    ring_step(0)
    r_away()
    cross_out(1, -1, 0)
    r_first()
    l_over_y(2)
    l_z(2)
    ring_step(1)
    l_y(-1, 1)
    retire(12)
    ring_step(2)
    l_over_y(3)
    l_z(3)
    ring_step(3)
    l_y(-2, 2)
    l_over_y(4)
    retire(30)

    def piece_of(n):
        source = (x + NX - n) % NX
        return gt.at[2 * (source % 2) + k, pl.ds(pl.multiple_of(source // 2 * 64, 64), 64)]

    cross[0].wait_recv()
    for h in (0, 1):
        for side in (0, 1):
            arrived[side, h].wait_recv()
        rows = pl.ds(pl.multiple_of(xh * 64 + h * 32, 32), 32)
        gt[2 * row + k, rows, :] = (
            half_term(0, h) + ring_r[0, h, 3].astype(F32) + ring_r[1, h, 3].astype(F32)
        ).astype(BF16)
    from_x = {n: send(piece_of(0), piece_of(0), at_x(n)) for n in (2, 1, 3)}
    passed = [send(piece_of(0), piece_of(0), sibling)]
    l_y(-3, 3)
    for n in (1, 3, 2):
        from_x[n].wait_recv()
        passed.append(send(piece_of(n), piece_of(n), sibling))
    r_second()
    for n in (-1, 1, -2, 2, -3, 3):
        for sign in (1, -1):
            l_from["f", sign, n].wait_recv()
    for sign in (1, -1, 2):
        l_from["y", sign, 4].wait_recv()
    for copy in passed:
        copy.wait_recv()

    gathered = {}
    for h in (0, 1):
        left = jnp.zeros((128, 256), F32)
        for q in range(4):
            left = left + lax.dot_general(
                gt[q], lbuf[q, :, h * 32:(h + 1) * 32, :].reshape(256, 1024), (((1,), (1,)), ((), ())),
                preferred_element_type=F32,
            )
        mbuf[h, y] = left.astype(BF16)
        gathered[h] = [send(mbuf.at[h, y], mbuf.at[h, y], at_y(n)) for n in (2, 1, 3)]
    r_core()
    retire(len(sent) - 10)
    r_end()

    met, far = {}, {}

    def sum_start(h):
        for side in (0, 1):
            sign = 1 - 2 * side
            if h == side:
                far_s[side] = partial(sign * 4, h).astype(BF16)
                far[side] = send(far_s.at[side], far_r.at[side], at_z(2 * sign))
            ring2_s[side, h, 0] = partial(sign * 3, h).astype(BF16)
            met[side, h] = send(ring2_s.at[side, h, 0], ring2_r.at[side, h, 0], at_z(sign))

    def sum_step(step, h):
        for side in (0, 1):
            sign = 1 - 2 * side
            total = partial(sign * (3 - step), h)
            met[side, h].wait_recv()
            total = total + ring2_r[side, h, step - 1].astype(F32)
            if step == 1 and h == side:
                far[side].wait_recv()
                total = total + far_r[side].astype(F32)
            ring2_s[side, h, step] = total.astype(BF16)
            met[side, h] = send(ring2_s.at[side, h, step], ring2_r.at[side, h, step], at_z(sign))

    for h in (0, 1):
        for copy in gathered[h]:
            copy.wait_recv()
        left_all = mbuf[h].reshape(512, 256)
        for n in range(2):
            right = rbuf[:, :, :, n * 512:(n + 1) * 512].reshape(512, 512)
            pf[h, :, :, n * 512:(n + 1) * 512] = lax.dot_general(
                left_all, right, (((0,), (0,)), ((), ())), preferred_element_type=F32
            ).reshape(8, 32, 512)
        sum_start(h)
    for step in (1, 2):
        for h in (0, 1):
            sum_step(step, h)

    def block(half, n, first=0, rows=64):
        start = (half * NZ + (z + n) % NZ) * 128 + k * 64 + first
        return out.at[pl.ds(pl.multiple_of(start, 16), rows)]

    into, across, crossed = {}, [], {}
    near, away_half = xh, 1 - xh

    def step_out(half, h, side, step):
        sign = 1 - 2 * side
        n = -sign * (step - 1)
        piece = block(half, n, 32 * h, 32)
        into[half is near, h, side, step] = send(piece, piece, at_z(sign))
        if step == 3:
            quarter = block(half, n, 32 * h + 16 * side, 16)
            into[half is near, h, side, 4] = send(quarter, quarter, at_z(2 * sign))

    def over_x(n):
        piece = block(near, n, 32, 32)
        crossed[n] = send(piece, piece, at_x(2))

    def over_core(half, n, first=0, rows=64):
        piece = block(half, n, first, rows)
        across.append(send(piece, piece, sibling))

    def mine(h):
        return final.at[pl.ds(h * 32, 32)], block(near, 0, 32 * h, 32)

    places = []
    for h in (0, 1):
        for side in (0, 1):
            met[side, h].wait_recv()
        final[h * 32:(h + 1) * 32, :] = (
            partial(0, h) + ring2_r[0, h, 2].astype(F32) + ring2_r[1, h, 2].astype(F32)
        ).astype(BF16)
        if h == 0:
            crossed["h0"] = send(*mine(0), at_x(2))
        places.append(load(*mine(h)))
    for h in (1, 0):
        for side in (0, 1):
            into[True, h, side, 1] = send(*mine(h), at_z(1 - 2 * side))
        if h == 1:
            crossed[0] = send(*mine(1), at_x(2))
    for h in (0, 1):
        across.append(send(*mine(h), sibling))

    def around(step):
        return (-step, step) if step < 4 else (4,)

    def own_class(h, step):
        for side in (0, 1):
            into[True, h, side, step].wait_recv()
            if step < 3:
                step_out(near, h, side, step + 1)
        if h == 1:
            for n in around(step):
                over_x(n)
        else:
            for n in around(step):
                over_core(near, n)

    def opposite(step):
        for side in (0, 1):
            into[False, 0, side, step].wait_recv()
            if step < 3:
                step_out(away_half, 0, side, step + 1)
        for n in around(step):
            over_core(away_half, n, 0, 32)

    def from_opposite(*offsets):
        for n in offsets:
            crossed[n].wait_recv()
            over_core(away_half, n, 32, 32)

    retire(len(sent) - 16)
    own_class(1, 1)
    crossed["h0"].wait_recv()
    for side in (0, 1):
        step_out(away_half, 0, side, 1)
    own_class(0, 1)
    over_core(away_half, 0, 0, 32)
    from_opposite(0)
    own_class(1, 2)
    opposite(1)
    own_class(0, 2)
    from_opposite(-1, 1)
    retire(len(sent) - 34)
    own_class(1, 3)
    opposite(2)
    own_class(1, 4)
    own_class(0, 3)
    from_opposite(-2, 2)
    opposite(3)
    own_class(0, 4)
    from_opposite(-3, 3)
    opposite(4)
    from_opposite(4)
    retire(len(sent) - 14)
    for copy in places:
        copy.wait()
    for copy in across:
        copy.wait_recv()
    for copy in sent:
        copy.wait_send()
    assert count[0] == COPIES, count[0]


def shards(out_grads, activations, output_factor, input_factor):
    vmem = pltpu.VMEM
    args = (out_grads, activations, output_factor, input_factor.T)
    dma = pltpu.SemaphoreType.DMA
    anywhere = pl.BlockSpec(memory_space=pl.ANY)
    hbm = pl.BlockSpec(memory_space=pltpu.HBM)
    return pl.pallas_call(
        kernel,
        out_shape=pltpu.VMEM((2048, 1024), BF16),
        in_specs=[hbm] * 4,
        out_specs=anywhere,
        scratch_shapes=[
            vmem((1280, 2048), BF16),
            vmem((1280, 1024), BF16),
            vmem((4, 256, 1024), F32),
            vmem((4, 256, 1024), BF16),
            vmem((4, 256, 1024), BF16),
            vmem((8, 64, 1024), BF16),
            vmem((8, 64, 1024), BF16),
            vmem((2, 2, 4, 32, 1024), BF16),
            vmem((2, 2, 4, 32, 1024), BF16),
            vmem((4, 128, 1024), BF16),
            vmem((4, 8, 64, 1024), BF16),
            vmem((4, 2, 64, 1024), BF16),
            vmem((64, 1024), BF16),
            vmem((2, 4, 128, 256), BF16),
            vmem((2, 8, 32, 1024), F32),
            vmem((2, 32, 1024), BF16),
            vmem((2, 32, 1024), BF16),
            vmem((2, 2, 3, 32, 1024), BF16),
            vmem((2, 2, 3, 32, 1024), BF16),
            vmem((64, 1024), BF16),
            dma((16,)), dma((COPIES,)), dma((COPIES,)), dma((11,)), dma((11,)),
        ],
        compiler_params=pltpu.CompilerParams(
            collective_id=0, has_side_effects=True, vmem_limit_bytes=40 * 2**20
        ),
    )(*(pltpu.with_memory_space_constraint(v, pltpu.HBM) for v in args))


def solution(mesh):
    placed = (P("dp", "row"), P("dp", "col"), P("row", "dp", None), P("col", ("dp", "row")))
    return jax.shard_map(
        shards, mesh=mesh, in_specs=placed, out_specs=P("row", "col"), check_vma=False
    )
```

```python
import functools

import jax
import jax.numpy as jnp
from jax import lax
from jax.experimental import pallas as pl
from jax.experimental.pallas import tpu as pltpu
from jax.sharding import PartitionSpec as P

NX, NY, NZ = 4, 4, 8
BF16, F32 = jnp.bfloat16, jnp.float32
COPIES = 146


def kernel(
    g_hbm, a_hbm, l_hbm, r_hbm, out,
    g_v, a_v, own, give, take, cross_s, cross_r, ring_s, ring_r, gt, lbuf, rbuf, r_mine, mbuf, pf, far_s, far_r, ring2_s, ring2_r, final,
    load_sem, send_sem, recv_sem, r_send, r_recv,
):
    d, row, y = lax.axis_index("dp"), lax.axis_index("row"), lax.axis_index("col")
    k, z, xh = d % 2, (d // 2) % NZ, d // (2 * NZ)
    x = 2 * xh + row

    def device(x, y, z, k):
        return {"dp": (x // 2) * (2 * NZ) + z * 2 + k, "row": x % 2, "col": y}

    def at_x(n, core=None):
        return device((x + n) % NX, y, z, k if core is None else core)

    def at_y(n):
        return device(x, (y + n) % NY, z, k)

    def at_z(n):
        return device(x, y, (z + n) % NZ, k)

    sibling = device(x, y, z, 1 - k)
    count = [0]
    sent = []

    def send(src, dst, target):
        i = count[0]
        count[0] += 1
        copy = pltpu.make_async_remote_copy(
            src_ref=src, dst_ref=dst, send_sem=send_sem.at[i], recv_sem=recv_sem.at[i],
            device_id=target, device_id_type=pl.DeviceIdType.MESH,
        )
        copy.start()
        sent.append(copy)
        return copy

    def retire(count):
        for copy in sent[:count]:
            copy.wait_send()
        del sent[:count]

    loads = []

    def load(src, dst):
        copy = pltpu.make_async_copy(src, dst, load_sem.at[len(loads)])
        copy.start()
        loads.append(copy)
        return copy

    home = z // 4
    load_a, load_g = {}, []

    def load_columns(n):
        part = pl.ds(pl.multiple_of((z + n) % 4 * 256, 256), 256)
        load_a[n] = load(a_hbm.at[:, part], a_v.at[:, part])

    load_columns(0)
    for n in range(4):
        part = pl.ds(pl.multiple_of((n // 2 + (1 - k)) % 2 * 1024 + n % 2 * 512, 512), 512)
        load_g.append(load(g_hbm.at[:, part], g_v.at[:, part]))
    for n in (3, 1, 2):
        load_columns(n)
    load_l = [load(l_hbm.at[0, :, pl.ds(q * 1024, 1024)], lbuf.at[q, z]) for q in range(4)]
    load_r = load(r_hbm, r_mine)

    barrier = pltpu.get_barrier_semaphore()
    partners = [at_z(1), at_z(-1), at_z(2), at_z(-2), at_z(4), sibling] + [at_y(n) for n in (1, 2, 3)]
    partners += [at_x(n, core) for n in (1, 2, 3) for core in (k, 1 - k)]
    for partner in partners:
        pl.semaphore_signal(barrier, inc=1, device_id=partner, device_id_type=pl.DeviceIdType.MESH)

    l_from = {}

    def l_block(q, n):
        return lbuf.at[q, (z + n) % NZ]

    def l_half(q, n, half):
        return lbuf.at[q, (z + n) % NZ, pl.ds(32 * half, 32)]

    def l_z(step):
        if step == 0:
            for sign in (1, -1):
                l_from[sign, 1] = send(l_block(y, 0), l_block(y, 0), at_z(sign))
            return
        for sign in (1, -1):
            n = -sign * step
            if step < 3:
                l_from[sign, step + 1] = send(l_block(y, n), l_block(y, n), at_z(sign))
            elif step == 3:
                half = 0 if sign == 1 else 1
                l_from[sign, 4] = send(l_half(y, n, half), l_half(y, n, half), at_z(sign))

    def l_over_y(step):
        for sign in (1, -1):
            l_from[sign, step].wait_recv()
        for n in ((-step, step) if step < 4 else (4,)):
            for sign in ((1, -1) if step < 4 else (1, -1, 2)):
                l_from["y", sign, n] = send(l_block(y, n), l_block(y, n), at_y(sign))

    def l_y(*offsets):
        for n in offsets:
            for sign in (1, -1):
                l_from["y", sign, n].wait_recv()
                half = 0 if sign == 1 else 1
                block = l_half((y + NY - sign) % NY, n, half)
                l_from["f", sign, n] = send(block, block, at_y(sign))

    def r_copy(src, dst, i, target):
        return pltpu.make_async_remote_copy(
            src_ref=src, dst_ref=dst, send_sem=r_send.at[i], recv_sem=r_recv.at[i],
            device_id=target, device_id_type=pl.DeviceIdType.MESH,
        )

    away = r_copy(r_mine, rbuf.at[2 * xh + home, row], 0, at_z(4))

    def pair(n):
        source = (x + NX - n) % NX
        return rbuf.at[pl.ds(source // 2 * 2, 2), source % 2]

    def slot(source, n):
        return rbuf.at[2 * (source // 2) + n, source % 2]

    own_spread = [r_copy(r_mine, slot(x, home), n, at_x(n)) for n in (1, 2, 3)]
    far_spread = [r_copy(slot(x, 1 - home), slot(x, 1 - home), 3 + n, at_x(n)) for n in (1, 2, 3)]
    handed = [r_copy(pair(n), pair(n), 7 + n, sibling) for n in range(4)]

    def r_first():
        @pl.when(k == home)
        def _():
            for copy in own_spread:
                copy.start()
            rbuf[2 * xh + home, row] = r_mine[...]

    def r_away():
        @pl.when(k != home)
        def _():
            away.start()

    def r_second():
        @pl.when(k == home)
        def _():
            away.wait_recv()
            for copy in far_spread:
                copy.start()
            handed[0].start()

    def r_core():
        @pl.when(k == home)
        def _():
            for n in (1, 2, 3):
                own_spread[n - 1].wait_recv()
                far_spread[n - 1].wait_recv()
                handed[n].start()

    def r_end():
        @pl.when(k == home)
        def _():
            for copy in own_spread + far_spread + handed:
                copy.wait_send()

        @pl.when(k != home)
        def _():
            away.wait_send()
            for copy in handed:
                copy.wait_recv()

    exchange = {}

    def term(q_off, core):
        q = (z + q_off) % 4
        a_part = a_v[:, pl.ds(pl.multiple_of(q * 256, 256), 256)]

        def part(half, n):
            start = pl.multiple_of(half * 1024 + n * 512, 512)
            return lax.dot_general(
                a_part, g_v[:, pl.ds(start, 512)], (((0,), (0,)), ((), ())), preferred_element_type=F32
            )

        if core == 0:
            for n in range(2):
                give[q, :, n * 512:(n + 1) * 512] = part(1 - k, n).astype(BF16)
        else:
            for n in range(2):
                own[q, :, n * 512:(n + 1) * 512] = part(k, n)

    def trade(q_off):
        q = (z + q_off) % 4
        exchange[q_off] = send(give.at[q], take.at[q], sibling)

    cross = {}

    def chip_term(n, first, rows):
        chunk = (z + n) % NZ
        rows = pl.ds(pl.multiple_of((chunk // 4) * 128 + first, rows), rows)
        return own[chunk % 4, rows, :] + take[chunk % 4, rows, :].astype(F32)

    def cross_out(*offsets):
        for n in offsets:
            cross_s[n % NZ] = chip_term(n, (1 - xh) * 64, 64).astype(BF16)
            cross[n % NZ] = send(cross_s.at[n % NZ], cross_r.at[n % NZ], at_x(2))

    def half_term(n, h):
        return chip_term(n, xh * 64 + h * 32, 32) + cross_r[n % NZ, h * 32:(h + 1) * 32, :].astype(F32)

    def partial(n, h):
        return pf[h, (z + n) % NZ]

    arrived = {}

    def ring_step(step):
        for sign in (1, -1)[:1 if step == 0 else 2]:
            cross[sign * (4 - step) % NZ].wait_recv()
        for h, side in ((0, 0), (1, 1), (1, 0), (0, 1)):
            sign = 1 - 2 * side
            if step == 0 and h != side:
                continue
            total = half_term(sign * (4 - step), h)
            if (side, h) in arrived:
                arrived[side, h].wait_recv()
                total = total + ring_r[side, h, step - 1].astype(F32)
            ring_s[side, h, step] = total.astype(BF16)
            arrived[side, h] = send(ring_s.at[side, h, step], ring_r.at[side, h, step], at_z(sign))

    load_a[0].wait()
    for copy in load_g[:2]:
        copy.wait()
    term(0, 0)
    for copy in load_l:
        copy.wait()
    load_r.wait()
    pl.semaphore_wait(barrier, len(partners))
    trade(0)
    l_z(0)
    for copy in load_g[2:]:
        copy.wait()
    term(0, 1)
    load_a[3].wait()
    term(3, 0)
    trade(3)
    exchange[0].wait_recv()
    cross_out(4)
    load_a[1].wait()
    load_a[2].wait()
    term(1, 0)
    trade(1)
    term(3, 1)
    exchange[3].wait_recv()
    cross_out(3)
    term(1, 1)
    exchange[1].wait_recv()
    cross_out(-3)
    l_over_y(1)
    l_z(1)
    term(2, 0)
    trade(2)
    term(2, 1)
    exchange[2].wait_recv()
    cross_out(2, -2)
    ring_step(0)
    r_away()
    cross_out(1, -1, 0)
    r_first()
    l_over_y(2)
    l_z(2)
    ring_step(1)
    l_y(-1, 1)
    retire(12)
    ring_step(2)
    l_over_y(3)
    l_z(3)
    ring_step(3)
    l_y(-2, 2)
    l_over_y(4)
    retire(30)

    def piece_of(n):
        source = (x + NX - n) % NX
        return gt.at[2 * (source % 2) + k, pl.ds(pl.multiple_of(source // 2 * 64, 64), 64)]

    cross[0].wait_recv()
    for h in (0, 1):
        for side in (0, 1):
            arrived[side, h].wait_recv()
        rows = pl.ds(pl.multiple_of(xh * 64 + h * 32, 32), 32)
        gt[2 * row + k, rows, :] = (
            half_term(0, h) + ring_r[0, h, 3].astype(F32) + ring_r[1, h, 3].astype(F32)
        ).astype(BF16)
    from_x = {n: send(piece_of(0), piece_of(0), at_x(n)) for n in (2, 1, 3)}
    passed = [send(piece_of(0), piece_of(0), sibling)]
    l_y(-3, 3)
    for n in (1, 3, 2):
        from_x[n].wait_recv()
        passed.append(send(piece_of(n), piece_of(n), sibling))
    r_second()
    for n in (-1, 1, -2, 2, -3, 3):
        for sign in (1, -1):
            l_from["f", sign, n].wait_recv()
    for sign in (1, -1, 2):
        l_from["y", sign, 4].wait_recv()
    for copy in passed:
        copy.wait_recv()

    gathered = {}
    for h in (0, 1):
        left = jnp.zeros((128, 256), F32)
        for q in range(4):
            left = left + lax.dot_general(
                gt[q], lbuf[q, :, h * 32:(h + 1) * 32, :].reshape(256, 1024), (((1,), (1,)), ((), ())),
                preferred_element_type=F32,
            )
        mbuf[h, y] = left.astype(BF16)
        gathered[h] = [send(mbuf.at[h, y], mbuf.at[h, y], at_y(n)) for n in (2, 1, 3)]
    r_core()
    retire(len(sent) - 10)
    r_end()

    met, far = {}, {}

    def sum_start(h):
        sign = 1 - 2 * h
        far_s[h] = partial(sign * 4, h).astype(BF16)
        far[h] = send(far_s.at[h], far_r.at[h], at_z(2 * sign))
        for side in (h, 1 - h):
            sign = 1 - 2 * side
            ring2_s[side, h, 0] = partial(sign * 3, h).astype(BF16)
            met[side, h] = send(ring2_s.at[side, h, 0], ring2_r.at[side, h, 0], at_z(sign))

    def sum_step(step, h):
        for side in (1 - h, h):
            sign = 1 - 2 * side
            total = partial(sign * (3 - step), h)
            met[side, h].wait_recv()
            total = total + ring2_r[side, h, step - 1].astype(F32)
            if step == 1 and h == side:
                far[side].wait_recv()
                total = total + far_r[side].astype(F32)
            ring2_s[side, h, step] = total.astype(BF16)
            met[side, h] = send(ring2_s.at[side, h, step], ring2_r.at[side, h, step], at_z(sign))

    for h in (0, 1):
        for copy in gathered[h]:
            copy.wait_recv()
        left_all = mbuf[h].reshape(512, 256)
        for n in range(2):
            right = rbuf[:, :, :, n * 512:(n + 1) * 512].reshape(512, 512)
            pf[h, :, :, n * 512:(n + 1) * 512] = lax.dot_general(
                left_all, right, (((0,), (0,)), ((), ())), preferred_element_type=F32
            ).reshape(8, 32, 512)
        sum_start(h)
    for step in (1, 2):
        for h in (0, 1):
            sum_step(step, h)

    def block(half, n, first=0, rows=64):
        start = (half * NZ + (z + n) % NZ) * 128 + k * 64 + first
        return out.at[pl.ds(pl.multiple_of(start, 16), rows)]

    into, across, crossed = {}, [], {}
    near, away_half = xh, 1 - xh

    def step_out(half, h, side, step):
        sign = 1 - 2 * side
        n = -sign * (step - 1)
        piece = block(half, n, 32 * h, 32)
        into[half is near, h, side, step] = send(piece, piece, at_z(sign))
        if step == 3:
            quarter = block(half, n, 32 * h + 16 * side, 16)
            into[half is near, h, side, 4] = send(quarter, quarter, at_z(2 * sign))

    def over_x(n):
        piece = block(near, n, 32, 32)
        crossed[n] = send(piece, piece, at_x(2))

    def over_core(half, n, first=0, rows=64):
        piece = block(half, n, first, rows)
        across.append(send(piece, piece, sibling))

    def mine(h):
        return final.at[pl.ds(h * 32, 32)], block(near, 0, 32 * h, 32)

    places = []
    for h in (0, 1):
        for side in (0, 1):
            met[side, h].wait_recv()
        final[h * 32:(h + 1) * 32, :] = (
            partial(0, h) + ring2_r[0, h, 2].astype(F32) + ring2_r[1, h, 2].astype(F32)
        ).astype(BF16)
        if h == 0:
            crossed["h0"] = send(*mine(0), at_x(2))
        places.append(load(*mine(h)))
    for h in (1, 0):
        for side in (0, 1):
            into[True, h, side, 1] = send(*mine(h), at_z(1 - 2 * side))
        if h == 1:
            crossed[0] = send(*mine(1), at_x(2))
    for h in (0, 1):
        across.append(send(*mine(h), sibling))

    def around(step):
        return (-step, step) if step < 4 else (4,)

    def own_class(h, step):
        for side in (0, 1):
            into[True, h, side, step].wait_recv()
            if step < 3:
                step_out(near, h, side, step + 1)
        if h == 1:
            for n in around(step):
                over_x(n)
        else:
            for n in around(step):
                over_core(near, n)

    def opposite(step):
        for side in (0, 1):
            into[False, 0, side, step].wait_recv()
            if step < 3:
                step_out(away_half, 0, side, step + 1)
        for n in around(step):
            over_core(away_half, n, 0, 32)

    def from_opposite(*offsets):
        for n in offsets:
            crossed[n].wait_recv()
            over_core(away_half, n, 32, 32)

    retire(len(sent) - 16)
    own_class(1, 1)
    crossed["h0"].wait_recv()
    for side in (0, 1):
        step_out(away_half, 0, side, 1)
    own_class(0, 1)
    over_core(away_half, 0, 0, 32)
    from_opposite(0)
    own_class(1, 2)
    opposite(1)
    own_class(0, 2)
    from_opposite(-1, 1)
    retire(len(sent) - 34)
    own_class(1, 3)
    opposite(2)
    own_class(1, 4)
    own_class(0, 3)
    from_opposite(-2, 2)
    opposite(3)
    own_class(0, 4)
    from_opposite(-3, 3)
    opposite(4)
    from_opposite(4)
    retire(len(sent) - 14)
    for copy in places:
        copy.wait()
    for copy in across:
        copy.wait_recv()
    for copy in sent:
        copy.wait_send()
    assert count[0] == COPIES, count[0]


def shards(out_grads, activations, output_factor, input_factor):
    vmem = pltpu.VMEM
    args = (out_grads, activations, output_factor, input_factor.T)
    dma = pltpu.SemaphoreType.DMA
    anywhere = pl.BlockSpec(memory_space=pl.ANY)
    hbm = pl.BlockSpec(memory_space=pltpu.HBM)
    return pl.pallas_call(
        kernel,
        out_shape=pltpu.VMEM((2048, 1024), BF16),
        in_specs=[hbm] * 4,
        out_specs=anywhere,
        scratch_shapes=[
            vmem((1280, 2048), BF16),
            vmem((1280, 1024), BF16),
            vmem((4, 256, 1024), F32),
            vmem((4, 256, 1024), BF16),
            vmem((4, 256, 1024), BF16),
            vmem((8, 64, 1024), BF16),
            vmem((8, 64, 1024), BF16),
            vmem((2, 2, 4, 32, 1024), BF16),
            vmem((2, 2, 4, 32, 1024), BF16),
            vmem((4, 128, 1024), BF16),
            vmem((4, 8, 64, 1024), BF16),
            vmem((4, 2, 64, 1024), BF16),
            vmem((64, 1024), BF16),
            vmem((2, 4, 128, 256), BF16),
            vmem((2, 8, 32, 1024), F32),
            vmem((2, 32, 1024), BF16),
            vmem((2, 32, 1024), BF16),
            vmem((2, 2, 3, 32, 1024), BF16),
            vmem((2, 2, 3, 32, 1024), BF16),
            vmem((64, 1024), BF16),
            dma((16,)), dma((COPIES,)), dma((COPIES,)), dma((11,)), dma((11,)),
        ],
        compiler_params=pltpu.CompilerParams(
            collective_id=0, has_side_effects=True, vmem_limit_bytes=40 * 2**20
        ),
    )(*(pltpu.with_memory_space_constraint(v, pltpu.HBM) for v in args))


def solution(mesh):
    placed = (P("dp", "row"), P("dp", "col"), P("row", "dp", None), P("col", ("dp", "row")))
    return jax.shard_map(
        shards, mesh=mesh, in_specs=placed, out_specs=P("row", "col"), check_vma=False
    )
```
